128 devices in a mesh: row: 8 (over y_hi, x), col: 16 (over y_lo, z, core).
Axes of the slice: x: 4, y: 4 (y_hi: 2, y_lo: 2; y = y_hi * 2 + y_lo), z: 4, core: 2. Of those that a mesh axis runs over, the one named last changes fastest.
Arguments:
- gate_out: bfloat16 [32, 512, 2048], P(None, 'row', 'col'), may hold values from -6 to 6
- gate_in: bfloat16 [32, 512, 2048], P(None, 'row', 'col'), may hold values from -6 to 6
- values: bfloat16 [32, 512, 2048], P(None, 'row', 'col'), may hold values from -6 to 6
- filter_spec: float32 [2, 32, 1024, 2048], P(None, 'row', 'col'), may hold values from -6 to 6
- skip: float32 [32], replicated, may hold values from -3 to 3
Outputs:
- gated_output: float32 [32, 512, 2048], P(None, 'row', 'col')
The draws below stay inside these ranges and needn't reach their ends.
All inputs are finite; a program needn't handle non-finite values.
Results may differ from the reference program's by a relative error of at most 0.0049.
Values may be sent and summed in bfloat16 or wider, within the bound.
No kernel may reach another device: no remote copies, remote signals or barrier semaphores. Data moves between devices by JAX's collectives and lax.ppermute only.
A program may use at most 128 MiB of HBM per device.

```python
import math
import jax
import jax.numpy as jnp
from jax import lax

CHANNELS = 32
ROWS = 1024
COLS = 2048
COL_OUTER = 64


def block_levels(rng, shape, cuts, low, largest):
    loudness, own = 1.0, jax.random.fold_in(rng, 6)
    for axis_at, shards_of in cuts:
        steps = jnp.exp(jax.random.uniform(jax.random.fold_in(own, axis_at), (shards_of,), jnp.float32, low / len(cuts), largest / len(cuts)))
        loudness = loudness * jnp.repeat(steps, shape[axis_at] // shards_of).reshape([-1 if axis == axis_at else 1 for axis in range(len(shape))])
    return loudness


def bell_draw(stream_key, extent, deviation, reach, pieces=(), kind=jnp.bfloat16):
    loudness = block_levels(stream_key, extent, pieces, -0.22, 0.18) if pieces else 1.0
    entries = jax.random.normal(stream_key, extent, jnp.float32) * deviation * loudness
    return jnp.minimum(jnp.maximum(entries, -reach), reach).astype(kind)


def setup_inputs(seed: int = 0) -> dict:
    splits = jax.random.split(jax.random.key(seed), 6)
    return {
        "gate_out": bell_draw(splits[0], (CHANNELS, ROWS // 2, COLS), 1.0, 6.0, ((1, 8), (2, 16))),
        "gate_in": bell_draw(splits[1], (CHANNELS, ROWS // 2, COLS), 1.0, 6.0, ((1, 8), (2, 16))),
        "values": bell_draw(splits[2], (CHANNELS, ROWS // 2, COLS), 1.0, 6.0, ((1, 8), (2, 16))),
        "filter_spec": bell_draw(splits[3], (2, CHANNELS, ROWS, COLS), 1.0, 6.0, ((1, 8), (2, 16)), jnp.float32),
        "skip": bell_draw(splits[4], (CHANNELS,), 1.0, 3.0, (), jnp.float32),
    }


HIGHEST_MODE = lax.Precision.HIGHEST
TWO_PI = 2.0 * math.pi


def angles(first_index, second_index, modulus):
    product = (first_index[:, None] * second_index[None, :]) % modulus
    return product.astype(jnp.float32) * (TWO_PI / modulus)


def rounded(array):
    return lax.optimization_barrier(array.astype(jnp.bfloat16)).astype(jnp.float32)


def matmul(left, right):
    return jnp.dot(left, right, precision=HIGHEST_MODE, preferred_element_type=jnp.float32)


def precise_einsum(form, left, right):
    return jnp.einsum(form, left, right, precision=HIGHEST_MODE, preferred_element_type=jnp.float32)


def col_tables():
    outer_len = COL_OUTER
    inner_len = COLS // COL_OUTER
    outer_index = jnp.arange(outer_len, dtype=jnp.int32)
    inner_index = jnp.arange(inner_len, dtype=jnp.int32)
    outer_angle = angles(outer_index, outer_index, outer_len)
    inner_angle = angles(inner_index, inner_index, inner_len)
    mid_angle = angles(outer_index, inner_index, COLS)
    return (rounded(jnp.cos(outer_angle)), rounded(jnp.sin(outer_angle)),
            rounded(jnp.cos(inner_angle)), rounded(jnp.sin(inner_angle)),
            jnp.cos(mid_angle)[:, :, None], jnp.sin(mid_angle)[:, :, None])


def col_forward(real_part, imag_part, tables):
    outer_cosines, outer_sines, inner_cos, inner_sin, mid_cos, mid_sin = tables
    outer_len = COL_OUTER
    inner_len = COLS // COL_OUTER
    width_all = real_part.shape[1]
    real_lattice = real_part.reshape(outer_len, inner_len, width_all)
    imaginary_lattice = imag_part.reshape(outer_len, inner_len, width_all)
    step_real = precise_einsum("ct,cux->tux", outer_cosines, real_lattice) + precise_einsum("ct,cux->tux", outer_sines, imaginary_lattice)
    step_imaginary = precise_einsum("ct,cux->tux", outer_cosines, imaginary_lattice) - precise_einsum("ct,cux->tux", outer_sines, real_lattice)
    middle_real = rounded(step_real * mid_cos + step_imaginary * mid_sin)
    middle_imaginary = rounded(step_imaginary * mid_cos - step_real * mid_sin)
    output_real = precise_einsum("qj,kqm->kjm", inner_cos, middle_real) + precise_einsum("qj,kqm->kjm", inner_sin, middle_imaginary)
    output_imaginary = precise_einsum("qj,kqm->kjm", inner_cos, middle_imaginary) - precise_einsum("qj,kqm->kjm", inner_sin, middle_real)
    return output_real.reshape(COLS, width_all), output_imaginary.reshape(COLS, width_all)


def col_inverse(real_part, imag_part, tables):
    outer_cosines, outer_sines, inner_cos, inner_sin, mid_cos, mid_sin = tables
    outer_len = COL_OUTER
    inner_len = COLS // COL_OUTER
    width_all = real_part.shape[1]
    real_lattice = real_part.reshape(outer_len, inner_len, width_all)
    imaginary_lattice = imag_part.reshape(outer_len, inner_len, width_all)
    step_real = precise_einsum("jq,kjm->kqm", inner_cos, real_lattice) - precise_einsum("jq,kjm->kqm", inner_sin, imaginary_lattice)
    step_imaginary = precise_einsum("jq,kjm->kqm", inner_cos, imaginary_lattice) + precise_einsum("jq,kjm->kqm", inner_sin, real_lattice)
    middle_real = rounded(step_real * mid_cos - step_imaginary * mid_sin)
    middle_imaginary = rounded(step_imaginary * mid_cos + step_real * mid_sin)
    output_real = precise_einsum("gj,gbf->jbf", outer_cosines, middle_real) - precise_einsum("gj,gbf->jbf", outer_sines, middle_imaginary)
    output_imaginary = precise_einsum("gj,gbf->jbf", outer_cosines, middle_imaginary) + precise_einsum("gj,gbf->jbf", outer_sines, middle_real)
    return output_real.reshape(COLS, width_all), output_imaginary.reshape(COLS, width_all)


def reference(gate_out, gate_in, values, filter_spec, skip):
    gated_input = gate_in.astype(jnp.float32) * values.astype(jnp.float32)
    freq_rows = jnp.arange(ROWS, dtype=jnp.int32)
    grid_rows = jnp.arange(ROWS // 2, dtype=jnp.int32)
    grid_cols = jnp.arange(COLS, dtype=jnp.int32)
    row_angle = angles(freq_rows, grid_rows, ROWS)
    row_cos = rounded(jnp.cos(row_angle))
    row_sin = rounded(jnp.sin(row_angle))
    tables = col_tables()
    twist_angle = angles(freq_rows, grid_cols, ROWS * COLS)
    twist_cos = jnp.cos(twist_angle)
    twist_sin = jnp.sin(twist_angle)
    scale_back = 1.0 / (ROWS * COLS)

    def one_channel(items):
        source, spec_real, spec_imag = items
        source = rounded(source)
        row_re = matmul(row_cos, source)
        row_im = -matmul(row_sin, source)
        tw_re = rounded(row_re * twist_cos + row_im * twist_sin)
        tw_im = rounded(row_im * twist_cos - row_re * twist_sin)
        sp_re, sp_im = col_forward(tw_re.T, tw_im.T, tables)
        sp_re = sp_re.T
        sp_im = sp_im.T
        pr_re = rounded(sp_re * spec_real - sp_im * spec_imag)
        pr_im = rounded(sp_re * spec_imag + sp_im * spec_real)
        bk_re, bk_im = col_inverse(pr_re.T, pr_im.T, tables)
        bk_re = bk_re.T
        bk_im = bk_im.T
        un_re = rounded(bk_re * twist_cos - bk_im * twist_sin)
        un_im = rounded(bk_im * twist_cos + bk_re * twist_sin)
        summed = matmul(row_cos.T, un_re) - matmul(row_sin.T, un_im)
        return summed * scale_back

    convolved = lax.map(one_channel, (gated_input, filter_spec[0], filter_spec[1]))
    return gate_out.astype(jnp.float32) * (convolved + skip[:, None, None] * gated_input)
```

```python
import math

import jax
import jax.numpy as jnp
import ml_dtypes
import numpy as np
from jax import lax
from jax.experimental import pallas as pl
from jax.experimental.pallas import tpu as pltpu
from jax.sharding import PartitionSpec as P

ROWS = 1024
COLS = 2048
OUTER = 64
INNER = 32
HALF = ROWS // 2
TOTAL = ROWS * COLS
LANES = 128
BLOCKS = 8
PER = HALF // BLOCKS
TWO_PI = 2.0 * math.pi
BF16 = jnp.bfloat16
F32 = jnp.float32


def grid_angle(first, second, modulus):
    product = (np.asarray(first, np.int64)[:, None] * np.asarray(second, np.int64)[None, :]) % modulus
    return product.astype(np.float32) * np.float32(TWO_PI / modulus)


def narrow(array):
    return np.asarray(array, np.float32).astype(ml_dtypes.bfloat16)


def row_table():
    angle = grid_angle(np.arange(HALF), np.arange(HALF), ROWS)
    cosines, sines = np.cos(angle), -np.sin(angle)
    sines[:, 0] = 1.0 - 2.0 * (np.arange(HALF) % 2)
    parts = np.stack([cosines, sines], 0).reshape(2, HALF, BLOCKS, PER).transpose(1, 2, 0, 3)
    return narrow(np.repeat(parts[:, :, :, None, :], 2, 3).reshape(HALF, BLOCKS * 2 * 2 * PER))


def outer_tables():
    near = grid_angle(np.arange(OUTER), np.arange(OUTER), OUTER)
    far = grid_angle(np.arange(OUTER) + 1, np.arange(OUTER), OUTER)
    c, s, cm, sm = np.cos(near), np.sin(near), np.cos(far), np.sin(far)
    return narrow(
        np.stack(
            [
                np.block([[c, s], [-s, c]]),
                np.block([[cm, -sm], [-sm, -cm]]),
                np.block([[c.T, -s.T], [s.T, c.T]]),
                np.block([[cm.T, -sm.T], [-sm.T, -cm.T]]),
            ]
        )
    )


def inner_tables():
    angle = grid_angle(np.arange(INNER), np.arange(INNER), INNER)
    c, s = np.kron(np.eye(4), np.cos(angle)), np.kron(np.eye(4), np.sin(angle))
    return narrow(np.stack([np.block([[c, s], [-s, c]]), np.block([[c, -s], [s, c]])]))


def middle_tables():
    angle = grid_angle(np.arange(OUTER + 1), np.arange(INNER), COLS).reshape(-1, 1)
    angle = np.broadcast_to(angle, (angle.shape[0], LANES))
    return np.stack([np.cos(angle), np.sin(angle)]).astype(np.float32)


def half_step_tables():
    place = np.broadcast_to(grid_angle(np.arange(LANES), [1], 2 * COLS), (LANES, LANES))
    block = np.broadcast_to(grid_angle(LANES * np.arange(16), [1], 2 * COLS), (16, LANES))
    both = [np.stack([np.cos(x), np.sin(x)]).astype(np.float32) for x in (place, block)]
    return both


def twist_base():
    angle = grid_angle(np.arange(HALF), np.arange(LANES), TOTAL)
    angle = angle.reshape(BLOCKS, PER, LANES).transpose(0, 2, 1)
    angle = np.concatenate([angle, angle], 2)
    return np.stack([np.cos(angle), np.sin(angle)]).astype(np.float32)


def filter_moves():
    moves = np.zeros((2, 272, 256), np.float32)
    for side in range(2):
        low, high = (0, 128) if side == 0 else (128, 0)
        for copy in range(2):
            for e in range(PER):
                lane = copy * PER + e
                moves[side, low + copy * PER + e, lane] = 1.0
                if e == 0:
                    moves[side, 256 + copy, 128 + lane] = 1.0
                else:
                    moves[side, high + copy * PER + PER - e, 128 + lane] = 1.0
    return narrow(moves)


def rotate(real, imag, cosine, sine):
    return real * cosine - imag * sine, imag * cosine + real * sine


def row_forward_body(x_ref, table_ref, base_ref, phase_ref, out_ref, turned_ref):
    block = pl.program_id(0)

    @pl.when(block == 0)
    def _():
        for chan in range(4):
            part = x_ref[:, chan].reshape(HALF, LANES)
            turned_ref[chan * LANES : (chan + 1) * LANES, :] = part.T

    sums = jnp.dot(turned_ref[...], table_ref[...], preferred_element_type=F32)
    first = lax.broadcasted_iota(jnp.int32, (LANES, LANES), 1) < PER
    cosine, sine = rotate(base_ref[0, 0], base_ref[1, 0], phase_ref[0, 0], phase_ref[1, 0])
    for pair in range(2):
        upper = sums[pair * 256 : pair * 256 + 128]
        lower = sums[pair * 256 + 128 : pair * 256 + 256]
        real = jnp.where(first, upper[:, :LANES], lower[:, :LANES])
        imag = jnp.where(first, upper[:, LANES:], lower[:, LANES:])
        real, imag = rotate(real, imag, cosine, -sine)
        place = block if pair == 0 else 15 - block
        out_ref[place, 0] = real.astype(BF16)
        out_ref[place, 1] = imag.astype(BF16)


def row_forward(x, table, base, phase):
    return pl.pallas_call(
        row_forward_body,
        grid=(BLOCKS,),
        in_specs=[
            pl.BlockSpec((8, 4, 64, LANES), lambda i: (0, 0, 0, 0)),
            pl.BlockSpec((HALF, 256), lambda i: (0, i)),
            pl.BlockSpec((2, 1, LANES, LANES), lambda i: (0, i, 0, 0)),
            pl.BlockSpec((2, 1, 1, LANES), lambda i: (0, i, 0, 0)),
        ],
        out_specs=pl.BlockSpec((16, 2, LANES, LANES), lambda i: (0, 0, 0, 0)),
        out_shape=jax.ShapeDtypeStruct((16, 2, LANES, LANES), BF16),
        scratch_shapes=[pltpu.VMEM((4 * LANES, HALF), BF16)],
        compiler_params=pltpu.CompilerParams(vmem_limit_bytes=24 * 1024 * 1024),
        cost_estimate=pl.CostEstimate(flops=1_100_000_000, bytes_accessed=5_000_000, transcendentals=0),
        name="row_forward",
    )(x, table, base, phase)


def filter_body(own_ref, got_ref, extra_ref, moves_ref, out_ref):
    for part in range(2):
        total = None
        for source, low, high in ((own_ref, 0, 128), (got_ref, 128, 256), (extra_ref, 256, 272)):
            term = lax.dot_general(
                source[part],
                moves_ref[low:high, :],
                (((0,), (0,)), ((), ())),
                preferred_element_type=F32,
            )
            total = term if total is None else total + term
        out_ref[0, part] = total[:, :LANES].astype(BF16)
        out_ref[1, part] = total[:, LANES:].astype(BF16)


def filter_layout(own, got, extra, moves):
    step = 256
    return pl.pallas_call(
        filter_body,
        grid=(COLS // step,),
        in_specs=[
            pl.BlockSpec((2, 128, step), lambda i: (0, 0, i)),
            pl.BlockSpec((2, 128, step), lambda i: (0, 0, i)),
            pl.BlockSpec((2, 16, step), lambda i: (0, 0, i)),
            pl.BlockSpec((272, 256), lambda i: (0, 0)),
        ],
        out_specs=pl.BlockSpec((2, 2, step, LANES), lambda i: (0, 0, i, 0)),
        out_shape=jax.ShapeDtypeStruct((2, 2, COLS, LANES), BF16),
        compiler_params=pltpu.CompilerParams(vmem_limit_bytes=16 * 1024 * 1024),
        cost_estimate=pl.CostEstimate(flops=600_000_000, bytes_accessed=5_000_000, transcendentals=0),
        name="filter_layout",
    )(own, got, extra, moves)


def column_body(
    y_ref, filt_ref, outer_ref, inner_ref, mid_ref, place_ref, block_ref, base_ref, phase_ref, special_ref,
    out_ref, wide_ref, work_ref,
):
    special = special_ref[...] > 0.5

    def spread(block, carry):
        rows = pl.ds(pl.multiple_of(block * LANES, LANES), LANES)
        real = y_ref[block, 0].astype(F32)
        imag = y_ref[block, 1].astype(F32)
        cosine, sine = rotate(
            place_ref[0], place_ref[1], block_ref[0, pl.ds(block, 1), :], block_ref[1, pl.ds(block, 1), :]
        )
        wide_ref[0, rows, :] = real
        wide_ref[1, rows, :] = jnp.where(special, 0.0, imag)
        wide_ref[2, rows, :] = jnp.where(special, imag * cosine, real)
        wide_ref[3, rows, :] = jnp.where(special, -imag * sine, imag)
        return carry

    lax.fori_loop(0, 16, spread, 0)

    def gather(ref, which, at):
        return ref[which, pl.ds(at, OUTER, stride=INNER), :].astype(BF16)

    def pair_of(ref, which, at):
        return jnp.concatenate(
            [
                jnp.concatenate([gather(ref, which, at), gather(ref, which + 1, at)], 0),
                jnp.concatenate([gather(ref, which, at + 1), gather(ref, which + 1, at + 1)], 0),
            ],
            1,
        )

    def outer_forward(step, carry):
        at = step * 2
        for side in range(2):
            sums = jnp.dot(outer_ref[side], pair_of(wide_ref, 2 * side, at), preferred_element_type=F32)
            for part in range(2):
                for shift in range(2):
                    work_ref[2 * side + part, pl.ds(at + shift, OUTER, stride=INNER), :] = sums[
                        part * OUTER : (part + 1) * OUTER, shift * LANES : (shift + 1) * LANES
                    ]
        return carry

    lax.fori_loop(0, INNER // 2, outer_forward, 0)

    def inner_step(step, carry):
        rows = pl.ds(pl.multiple_of(step * LANES, LANES), LANES)
        turns = []
        for side in range(2):
            at = pl.ds(pl.multiple_of(step * LANES + side * INNER, INNER), LANES)
            turns.append((mid_ref[0, at, :], mid_ref[1, at, :]))
        sides = []
        for side in range(2):
            real, imag = rotate(
                work_ref[2 * side, rows, :], work_ref[2 * side + 1, rows, :], turns[side][0], -turns[side][1]
            )
            sides.append(jnp.concatenate([real.astype(BF16), imag.astype(BF16)], 0))
        spectrum = jnp.dot(inner_ref[0], jnp.concatenate(sides, 1), preferred_element_type=F32)
        sides = []
        for side in range(2):
            lanes = slice(side * LANES, (side + 1) * LANES)
            real, imag = rotate(
                spectrum[:LANES, lanes],
                spectrum[LANES:, lanes],
                filt_ref[side, 0, rows, :].astype(F32),
                filt_ref[side, 1, rows, :].astype(F32),
            )
            sides.append(jnp.concatenate([real.astype(BF16), imag.astype(BF16)], 0))
        middle = jnp.dot(inner_ref[1], jnp.concatenate(sides, 1), preferred_element_type=F32)
        for side in range(2):
            lanes = slice(side * LANES, (side + 1) * LANES)
            real, imag = rotate(middle[:LANES, lanes], middle[LANES:, lanes], turns[side][0], turns[side][1])
            work_ref[2 * side, rows, :] = real
            work_ref[2 * side + 1, rows, :] = imag
        return carry

    lax.fori_loop(0, 16, inner_step, 0)

    def outer_inverse(step, carry):
        at = step * 2
        near = jnp.dot(outer_ref[2], pair_of(work_ref, 0, at), preferred_element_type=F32)
        far = jnp.dot(outer_ref[3], pair_of(work_ref, 2, at), preferred_element_type=F32)
        for shift in range(2):
            lanes = slice(shift * LANES, (shift + 1) * LANES)
            near_re, near_im = near[:OUTER, lanes], near[OUTER:, lanes]
            far_re, far_im = far[:OUTER, lanes], far[OUTER:, lanes]
            rows = pl.ds(at + shift, OUTER, stride=INNER)
            wide_ref[0, rows, :] = jnp.where(special, near_re, near_re + far_re)
            wide_ref[1, rows, :] = jnp.where(special, far_re, near_im + far_im)
            wide_ref[2, rows, :] = far_im
        return carry

    lax.fori_loop(0, INNER // 2, outer_inverse, 0)

    def finish(block, carry):
        rows = pl.ds(pl.multiple_of(block * LANES, LANES), LANES)
        cosine, sine = rotate(
            place_ref[0], place_ref[1], block_ref[0, pl.ds(block, 1), :], block_ref[1, pl.ds(block, 1), :]
        )
        real = wide_ref[0, rows, :]
        imag = wide_ref[1, rows, :]
        imag = jnp.where(special, imag * cosine - wide_ref[2, rows, :] * sine, imag)
        cosine, sine = rotate(
            base_ref[0], base_ref[1], phase_ref[0, pl.ds(block, 1), :], phase_ref[1, pl.ds(block, 1), :]
        )
        real, imag = rotate(real, imag, cosine, sine)
        out_ref[block, 0] = real.astype(BF16)
        out_ref[block, 1] = imag.astype(BF16)
        return carry

    lax.fori_loop(0, 16, finish, 0)


def column_step(y, filt, outer, inner, mid, place, block, base, phase, special):
    whole = pl.BlockSpec(memory_space=pltpu.VMEM)
    return pl.pallas_call(
        column_body,
        in_specs=[whole] * 10,
        out_specs=whole,
        out_shape=jax.ShapeDtypeStruct((16, 2, LANES, LANES), BF16),
        scratch_shapes=[pltpu.VMEM((4, COLS, LANES), F32), pltpu.VMEM((4, COLS, LANES), F32)],
        compiler_params=pltpu.CompilerParams(vmem_limit_bytes=32 * 1024 * 1024),
        cost_estimate=pl.CostEstimate(flops=2_000_000_000, bytes_accessed=9_000_000, transcendentals=0),
        name="column_step",
    )(y, filt, outer, inner, mid, place, block, base, phase, special)


def row_inverse_body(z_ref, table_ref, out_ref, split_ref):
    @pl.when(pl.program_id(0) == 0)
    def _():
        first = lax.broadcasted_iota(jnp.int32, (LANES, LANES), 1) < PER
        for place in range(16):
            pair, block = (0, place) if place < 8 else (1, 15 - place)
            for part in range(2):
                values = z_ref[place, part]
                lanes = slice((block * 2 + part) * LANES, (block * 2 + part + 1) * LANES)
                zero = jnp.zeros_like(values)
                split_ref[pair * 256 : pair * 256 + 128, lanes] = jnp.where(first, values, zero)
                split_ref[pair * 256 + 128 : pair * 256 + 256, lanes] = jnp.where(first, zero, values)

    sums = lax.dot_general(
        table_ref[...], split_ref[...], (((1,), (1,)), ((), ())), preferred_element_type=F32
    ) * (1.0 / TOTAL)
    for row in range(2):
        for chan in range(4):
            out_ref[row, chan] = sums[row * 64 : (row + 1) * 64, chan * LANES : (chan + 1) * LANES].astype(BF16)


def row_inverse(z, table):
    return pl.pallas_call(
        row_inverse_body,
        grid=(4,),
        in_specs=[
            pl.BlockSpec((16, 2, LANES, LANES), lambda i: (0, 0, 0, 0)),
            pl.BlockSpec((LANES, COLS), lambda i: (i, 0)),
        ],
        out_specs=pl.BlockSpec((2, 4, 64, LANES), lambda i: (i, 0, 0, 0)),
        out_shape=jax.ShapeDtypeStruct((8, 4, 64, LANES), BF16),
        scratch_shapes=[pltpu.VMEM((4 * LANES, COLS), BF16)],
        compiler_params=pltpu.CompilerParams(vmem_limit_bytes=16 * 1024 * 1024),
        cost_estimate=pl.CostEstimate(flops=1_100_000_000, bytes_accessed=4_000_000, transcendentals=0),
        name="row_inverse",
    )(z, table)


def turn(first, second, modulus):
    angle = ((first * second) % modulus).astype(F32) * (TWO_PI / modulus)
    return jnp.stack([jnp.cos(angle), jnp.sin(angle)])


def per_device(gate_out, gate_in, values, filter_spec, skip):
    col = lax.axis_index("col")
    low_side = col < 8
    table = jnp.asarray(row_table())

    gated = gate_in.astype(F32) * values.astype(F32)
    x = lax.all_to_all(gated.astype(BF16), "row", split_axis=0, concat_axis=0, tiled=True)

    mine = jnp.where(low_side, 0, 2)
    own = lax.dynamic_slice_in_dim(filter_spec, mine, 2, axis=1).astype(BF16)
    other = lax.dynamic_slice_in_dim(filter_spec, 2 - mine, 2, axis=1).astype(BF16)
    got = lax.ppermute(other, "col", [(i, 15 - i) for i in range(16)])
    extra_low = lax.ppermute(
        filter_spec[:, :2, 0, :].astype(BF16), "col", [(i, (16 - i) % 8) for i in range(8, 16)]
    )
    extra_high = lax.ppermute(
        filter_spec[:, 2:, 0, :].astype(BF16), "col", [(i, 8 + (i - 1) % 8) for i in range(8, 16)]
    )
    extra = jnp.where(low_side, extra_low, extra_high)
    extra = jnp.pad(extra, ((0, 0), (0, 14), (0, 0)))
    moves = jnp.where(low_side, filter_moves()[0], filter_moves()[1])
    filt = filter_layout(own.reshape(2, 128, COLS), got.reshape(2, 128, COLS), extra, moves)

    lane = jnp.arange(LANES, dtype=jnp.int32) % PER
    all_k1 = (PER * jnp.arange(BLOCKS, dtype=jnp.int32))[:, None, None] + lane[None, None, :]
    y = row_forward(x.reshape(8, 4, 64, LANES), table, twist_base(), turn(all_k1, col, ROWS * 16))
    y = lax.all_to_all(y, "col", split_axis=0, concat_axis=0, tiled=True)

    own_k1 = PER * jnp.where(low_side, col, 15 - col) + lane
    place, block = half_step_tables()
    base = turn(jnp.arange(LANES, dtype=jnp.int32)[:, None], own_k1[None, :], TOTAL)
    phase = turn(jnp.arange(16, dtype=jnp.int32)[:, None], own_k1[None, :], ROWS * 16)
    special = (own_k1 == 0).astype(F32)[None, :]
    z = column_step(
        y, filt, outer_tables(), inner_tables(), middle_tables(), place, block, base, phase, special
    )
    z = lax.all_to_all(z, "col", split_axis=0, concat_axis=0, tiled=True)

    convolved = row_inverse(z, table).reshape(32, 64, LANES)
    convolved = lax.all_to_all(convolved, "row", split_axis=0, concat_axis=0, tiled=True)
    return gate_out.astype(F32) * (convolved.astype(F32) + skip[:, None, None] * gated)


def solution(mesh):
    return jax.shard_map(
        per_device,
        mesh=mesh,
        in_specs=(
            P(None, "row", "col"),
            P(None, "row", "col"),
            P(None, "row", "col"),
            P(None, "row", "col", None),
            P(),
        ),
        out_specs=P(None, "row", "col"),
        check_vma=False,
    )
```

```python
import math

import jax
import jax.numpy as jnp
import ml_dtypes
import numpy as np
from jax import lax
from jax.experimental import pallas as pl
from jax.experimental.pallas import tpu as pltpu
from jax.sharding import PartitionSpec as P

ROWS = 1024
COLS = 2048
OUTER = 64
INNER = 32
HALF = ROWS // 2
TOTAL = ROWS * COLS
LANES = 128
BLOCKS = 8
PER = HALF // BLOCKS
TWO_PI = 2.0 * math.pi
BF16 = jnp.bfloat16
F32 = jnp.float32


def grid_angle(first, second, modulus):
    product = (np.asarray(first, np.int64)[:, None] * np.asarray(second, np.int64)[None, :]) % modulus
    return product.astype(np.float32) * np.float32(TWO_PI / modulus)


def narrow(array):
    return np.asarray(array, np.float32).astype(ml_dtypes.bfloat16)


def row_table():
    angle = grid_angle(np.arange(HALF), np.arange(HALF), ROWS)
    cosines, sines = np.cos(angle), -np.sin(angle)
    sines[:, 0] = 1.0 - 2.0 * (np.arange(HALF) % 2)
    parts = np.stack([cosines, sines], 0).reshape(2, HALF, BLOCKS, PER).transpose(1, 2, 0, 3)
    return narrow(np.repeat(parts[:, :, :, None, :], 2, 3).reshape(HALF, BLOCKS * 2 * 2 * PER))


def pair_order(table, first, second):
    rows, cols = table.shape[0] // 2, table.shape[1] // 2
    out = np.zeros((2, rows // first, 2, first, 2, cols // second, 2, second), np.float32)
    for which in range(2):
        out[:, :, which, :, :, :, which, :] = table.reshape(2, rows // first, first, 2, cols // second, second)
    return out.reshape(4 * rows, 4 * cols)


def outer_tables():
    near = grid_angle(np.arange(OUTER), np.arange(OUTER), OUTER)
    far = grid_angle(np.arange(OUTER) + 1, np.arange(OUTER), OUTER)
    c, s, cm, sm = np.cos(near), np.sin(near), np.cos(far), np.sin(far)
    return [
        pair_order(np.block([[c, s], [-s, c]]), 1, 4),
        pair_order(np.block([[cm, -sm], [-sm, -cm]]), 1, 4),
        pair_order(np.block([[c.T, -s.T], [s.T, c.T]]), 4, 1),
        pair_order(np.block([[cm.T, -sm.T], [-sm.T, -cm.T]]), 4, 1),
    ]


def inner_tables():
    angle = grid_angle(np.arange(INNER), np.arange(INNER), INNER)
    c, s = np.cos(angle), np.sin(angle)
    spread = np.zeros((2, 4, INNER, 2, INNER // 2, 4, 2), np.float32)
    for k in range(4):
        spread[:, k, :, :, :, k, :] = np.block([[c, s], [-s, c]]).reshape(2, INNER, 2, INNER // 2, 2)
    spread = spread.reshape(256, 256)
    return [spread, spread.T]


def step_tables():
    return narrow(np.stack(outer_tables() + inner_tables()))


def middle_tables():
    angle = grid_angle(np.arange(OUTER + 1), np.arange(INNER), COLS)
    sides = []
    for side in range(2):
        own = angle[side : side + OUTER].reshape(16, 4, 16, 2).transpose(0, 2, 1, 3).reshape(COLS, 1)
        own = np.broadcast_to(own, (COLS, LANES))
        sides.append(np.stack([np.cos(own), np.sin(own)]))
    return np.stack(sides).astype(np.float32)


def place_order():
    return np.arange(LANES).reshape(4, INNER).T.reshape(-1)


def place_moves():
    return narrow(np.eye(LANES)[place_order()])


def twist_base():
    angle = grid_angle(np.arange(HALF), place_order(), TOTAL)
    angle = angle.reshape(BLOCKS, PER, LANES).transpose(0, 2, 1)
    angle = np.concatenate([angle, angle], 2)
    return np.stack([np.cos(angle), np.sin(angle)]).astype(np.float32)


def filter_moves():
    moves = np.zeros((2, 272, 256), np.float32)
    for side in range(2):
        low, high = (0, 128) if side == 0 else (128, 0)
        for copy in range(2):
            for e in range(PER):
                lane = copy * PER + e
                moves[side, low + copy * PER + e, lane] = 1.0
                if e == 0:
                    moves[side, 256 + copy, 128 + lane] = 1.0
                else:
                    moves[side, high + copy * PER + PER - e, 128 + lane] = 1.0
    return narrow(moves)


def rotate(real, imag, cosine, sine):
    return real * cosine - imag * sine, imag * cosine + real * sine


def row_forward_body(x_hbm, table_ref, twist_ref, order_ref, out_hbm, x_ref, turned_ref, out_ref, sems):
    loads = []
    for chan in range(4):
        loads.append(pltpu.make_async_copy(x_hbm.at[:, chan], x_ref.at[chan], sems.at[chan]))
        loads[-1].start()
    for chan in range(4):
        loads[chan].wait()
        turned_ref[chan * LANES : (chan + 1) * LANES, :] = lax.dot_general(
            order_ref[...],
            x_ref[chan].reshape(HALF, LANES),
            (((1,), (1,)), ((), ())),
            preferred_element_type=F32,
        ).astype(BF16)

    first = lax.broadcasted_iota(jnp.int32, (LANES, LANES), 1) < PER
    stores = []
    for block in range(BLOCKS):
        sums = jnp.dot(
            turned_ref[...], table_ref[:, block * 256 : (block + 1) * 256], preferred_element_type=F32
        )
        cosine, sine = twist_ref[0, block], twist_ref[1, block]
        for pair in range(2):
            upper = sums[pair * 256 : pair * 256 + 128]
            lower = sums[pair * 256 + 128 : pair * 256 + 256]
            real = jnp.where(first, upper[:, :LANES], lower[:, :LANES])
            imag = jnp.where(first, upper[:, LANES:], lower[:, LANES:])
            real, imag = rotate(real, imag, cosine, -sine)
            place = block if pair == 0 else 15 - block
            out_ref[place, 0] = real.astype(BF16)
            out_ref[place, 1] = imag.astype(BF16)
            stores.append(pltpu.make_async_copy(out_ref.at[place], out_hbm.at[place], sems.at[4 + place]))
            stores[-1].start()
    for copy in stores:
        copy.wait()


def row_forward(x, table, twist, order):
    anywhere = pl.BlockSpec(memory_space=pl.ANY)
    inside = pl.BlockSpec(memory_space=pltpu.VMEM)
    block = (16, 2, LANES, LANES)
    return pl.pallas_call(
        row_forward_body,
        in_specs=[anywhere, inside, inside, inside],
        out_specs=anywhere,
        out_shape=jax.ShapeDtypeStruct(block, BF16),
        scratch_shapes=[
            pltpu.VMEM((4, 8, 64, LANES), BF16),
            pltpu.VMEM((4 * LANES, HALF), BF16),
            pltpu.VMEM(block, BF16),
            pltpu.SemaphoreType.DMA((20,)),
        ],
        compiler_params=pltpu.CompilerParams(vmem_limit_bytes=16 * 1024 * 1024),
        cost_estimate=pl.CostEstimate(flops=1_100_000_000, bytes_accessed=5_000_000, transcendentals=0),
        name="row_forward",
    )(x, table, twist, order)


def filter_send_body(half_ref, spec_ref, out_ref):
    out_ref[...] = spec_ref[...].astype(BF16)


def filter_send(spec, half):
    return pl.pallas_call(
        filter_send_body,
        grid_spec=pltpu.PrefetchScalarGridSpec(
            num_scalar_prefetch=1,
            grid=(4,),
            in_specs=[pl.BlockSpec((1, 1, 64, COLS), lambda i, half: (i // 2, 2 * half[0] + i % 2, 0, 0))],
            out_specs=pl.BlockSpec((1, 1, 64, COLS), lambda i, half: (i // 2, i % 2, 0, 0)),
        ),
        out_shape=jax.ShapeDtypeStruct((2, 2, 64, COLS), BF16),
        compiler_params=pltpu.CompilerParams(vmem_limit_bytes=16 * 1024 * 1024),
        cost_estimate=pl.CostEstimate(flops=0, bytes_accessed=3_000_000, transcendentals=0),
        name="filter_send",
    )(half, spec)


def filter_body(half_ref, own_ref, got_ref, extra_ref, moves_ref, out_ref):
    for part in range(2):
        own = own_ref[part].reshape(LANES, own_ref.shape[3]).astype(BF16)
        total = None
        for source, low, high in ((own, 0, 128), (got_ref[part], 128, 256), (extra_ref[part], 256, 272)):
            term = lax.dot_general(
                source, moves_ref[low:high, :], (((0,), (0,)), ((), ())), preferred_element_type=F32
            )
            total = term if total is None else total + term
        out_ref[0, part] = total[:, :LANES].astype(BF16)
        out_ref[1, part] = total[:, LANES:].astype(BF16)


def filter_layout(spec, half, got, extra, moves):
    step = 512
    return pl.pallas_call(
        filter_body,
        grid_spec=pltpu.PrefetchScalarGridSpec(
            num_scalar_prefetch=1,
            grid=(COLS // step,),
            in_specs=[
                pl.BlockSpec((2, 2, 64, step), lambda i, half: (0, half[0], 0, i)),
                pl.BlockSpec((2, 128, step), lambda i, half: (0, 0, i)),
                pl.BlockSpec((2, 16, step), lambda i, half: (0, 0, i)),
                pl.BlockSpec((272, 256), lambda i, half: (0, 0)),
            ],
            out_specs=pl.BlockSpec((2, 2, step, LANES), lambda i, half: (0, 0, i, 0)),
        ),
        out_shape=jax.ShapeDtypeStruct((2, 2, COLS, LANES), BF16),
        compiler_params=pltpu.CompilerParams(vmem_limit_bytes=24 * 1024 * 1024),
        cost_estimate=pl.CostEstimate(flops=600_000_000, bytes_accessed=5_000_000, transcendentals=0),
        name="filter_layout",
    )(half, spec, got, extra, moves)


def column_body(
    y_hbm, turn_hbm, filt_hbm, step_hbm, mid_hbm, special_ref, out_hbm,
    y_ref, turn_ref, filt_ref, step_ref, mid_ref, work_ref, out_ref, sems,
):
    copies = []

    def fetch(source, target):
        copies.append(pltpu.make_async_copy(source, target, sems.at[len(copies)]))
        copies[-1].start()
        return copies[-1]

    step_copy = fetch(step_hbm, step_ref)
    in_copies = []
    for part in range(4):
        rows = pl.ds(part * 32, 32)
        in_copies.append(
            (
                fetch(y_hbm.at[:, :, rows], y_ref.at[:, :, rows]),
                fetch(turn_hbm.at[:, :, rows], turn_ref.at[:, :, rows]),
            )
        )
    mid_copies = []
    for part in range(2):
        rows = pl.ds(part * 1024, 1024)
        mid_copies.append(
            (
                fetch(mid_hbm.at[:, :, rows], mid_ref.at[:, :, rows]),
                fetch(filt_hbm.at[:, :, rows], filt_ref.at[:, :, rows]),
            )
        )

    special = special_ref[...] > 0.5
    step_copy.wait()

    def outer_forward(step):
        if step % 2 == 0:
            for copy in in_copies[step // 2]:
                copy.wait()
        rows = slice(step * 16, step * 16 + 16)
        parts = [[], [], [], []]
        for block in range(16):
            real = y_ref[block, 0, rows, :].astype(F32)
            imag = y_ref[block, 1, rows, :].astype(F32)
            parts[0].append(real)
            parts[1].append(jnp.where(special, 0.0, imag))
            parts[2].append(jnp.where(special, imag * turn_ref[0, block, rows, :], real))
            parts[3].append(jnp.where(special, imag * turn_ref[1, block, rows, :], imag))
        for side in range(2):
            data = [
                jnp.concatenate(
                    [x[half * 8 : half * 8 + 8] for x in parts[2 * side] + parts[2 * side + 1]], 0
                ).astype(BF16)
                for half in range(2)
            ]
            sums = jnp.dot(step_ref[side], jnp.concatenate(data, 1), preferred_element_type=F32)
            for part in range(2):
                for group in range(16):
                    for half in range(2):
                        at = group * LANES + step * 16 + half * 8
                        work_ref[2 * side + part, at : at + 8, :] = sums[
                            part * LANES + group * 8 : part * LANES + group * 8 + 8,
                            half * LANES : (half + 1) * LANES,
                        ]

    def inner_step(step):
        if step % 8 == 0:
            for copy in mid_copies[step // 8]:
                copy.wait()
        rows = slice(step * LANES, (step + 1) * LANES)
        sides = []
        for side in range(2):
            real, imag = rotate(
                work_ref[2 * side, rows, :],
                work_ref[2 * side + 1, rows, :],
                mid_ref[side, 0, rows, :],
                -mid_ref[side, 1, rows, :],
            )
            sides.append(jnp.concatenate([real.astype(BF16), imag.astype(BF16)], 0))
        spectrum = jnp.dot(step_ref[4], jnp.concatenate(sides, 1), preferred_element_type=F32)
        sides = []
        for side in range(2):
            lanes = slice(side * LANES, (side + 1) * LANES)
            real, imag = rotate(
                spectrum[:LANES, lanes],
                spectrum[LANES:, lanes],
                filt_ref[side, 0, rows, :].astype(F32),
                filt_ref[side, 1, rows, :].astype(F32),
            )
            sides.append(jnp.concatenate([real.astype(BF16), imag.astype(BF16)], 0))
        middle = jnp.dot(step_ref[5], jnp.concatenate(sides, 1), preferred_element_type=F32)
        for side in range(2):
            lanes = slice(side * LANES, (side + 1) * LANES)
            real, imag = rotate(
                middle[:LANES, lanes], middle[LANES:, lanes], mid_ref[side, 0, rows, :], mid_ref[side, 1, rows, :]
            )
            work_ref[2 * side, rows, :] = real
            work_ref[2 * side + 1, rows, :] = imag

    def outer_inverse(step):
        rows = slice(step * 16, step * 16 + 16)
        sums = []
        for side in range(2):
            data = []
            for half in range(2):
                pieces = []
                for part in range(2):
                    for group in range(16):
                        at = group * LANES + step * 16 + half * 8
                        pieces.append(work_ref[2 * side + part, at : at + 8, :])
                data.append(jnp.concatenate(pieces, 0).astype(BF16))
            sums.append(jnp.dot(step_ref[2 + side], jnp.concatenate(data, 1), preferred_element_type=F32))
        near, far = sums
        for block in range(16):

            def both(sums, part):
                at = part * LANES + block * 8
                return jnp.concatenate([sums[at : at + 8, :LANES], sums[at : at + 8, LANES:]], 0)

            near_re, near_im, far_re, far_im = both(near, 0), both(near, 1), both(far, 0), both(far, 1)
            cosine, sine = turn_ref[0, block, rows, :], turn_ref[1, block, rows, :]
            total_re, total_im = near_re + far_re, near_im + far_im
            real = jnp.where(special, near_re, total_re * cosine - total_im * sine)
            imag = jnp.where(special, far_re, total_im) * cosine + jnp.where(special, far_im, total_re) * sine
            out_ref[block, 0, rows, :] = real.astype(BF16)
            out_ref[block, 1, rows, :] = imag.astype(BF16)

    for step in range(8):
        outer_forward(step)
    for step in range(16):
        inner_step(step)
    out_copies = []
    for step in range(8):
        outer_inverse(step)
        if step % 2 == 1:
            rows = pl.ds((step - 1) * 16, 32)
            out_copies.append(fetch(out_ref.at[:, :, rows], out_hbm.at[:, :, rows]))
    for copy in out_copies:
        copy.wait()


def column_step(y, turns, filt, steps, mid, special):
    anywhere = pl.BlockSpec(memory_space=pl.ANY)
    block = (16, 2, LANES, LANES)
    return pl.pallas_call(
        column_body,
        in_specs=[anywhere] * 5 + [pl.BlockSpec(memory_space=pltpu.VMEM)],
        out_specs=anywhere,
        out_shape=jax.ShapeDtypeStruct(block, BF16),
        scratch_shapes=[
            pltpu.VMEM(block, BF16),
            pltpu.VMEM((2, 16, LANES, LANES), F32),
            pltpu.VMEM((2, 2, COLS, LANES), BF16),
            pltpu.VMEM((6, 256, 256), BF16),
            pltpu.VMEM((2, 2, COLS, LANES), F32),
            pltpu.VMEM((4, COLS, LANES), F32),
            pltpu.VMEM(block, BF16),
            pltpu.SemaphoreType.DMA((17,)),
        ],
        compiler_params=pltpu.CompilerParams(vmem_limit_bytes=60 * 1024 * 1024),
        cost_estimate=pl.CostEstimate(flops=2_000_000_000, bytes_accessed=10_000_000, transcendentals=0),
        name="column_step",
    )(y, turns, filt, steps, mid, special)


def row_inverse_body(z_ref, table_ref, order_ref, out_ref, split_ref):
    first = lax.broadcasted_iota(jnp.int32, (LANES, LANES), 1) < PER
    for place in range(16):
        pair, block = (0, place) if place < 8 else (1, 15 - place)
        for part in range(2):
            values = z_ref[place, part]
            lanes = slice((block * 2 + part) * LANES, (block * 2 + part + 1) * LANES)
            zero = jnp.zeros_like(values)
            split_ref[pair * 256 : pair * 256 + 128, lanes] = jnp.where(first, values, zero)
            split_ref[pair * 256 + 128 : pair * 256 + 256, lanes] = jnp.where(first, zero, values)

    for chan in range(4):
        sums = lax.dot_general(
            table_ref[...],
            split_ref[chan * LANES : (chan + 1) * LANES, :],
            (((1,), (1,)), ((), ())),
            preferred_element_type=F32,
        ) * (1.0 / TOTAL)
        sums = jnp.dot(sums.astype(BF16), order_ref[...], preferred_element_type=F32).astype(BF16)
        for row in range(8):
            out_ref[row, chan] = sums[row * 64 : (row + 1) * 64]


def row_inverse(z, table, order):
    inside = pl.BlockSpec(memory_space=pltpu.VMEM)
    return pl.pallas_call(
        row_inverse_body,
        in_specs=[inside] * 3,
        out_specs=inside,
        out_shape=jax.ShapeDtypeStruct((8, 4, 64, LANES), BF16),
        scratch_shapes=[pltpu.VMEM((4 * LANES, COLS), BF16)],
        compiler_params=pltpu.CompilerParams(vmem_limit_bytes=16 * 1024 * 1024),
        cost_estimate=pl.CostEstimate(flops=1_100_000_000, bytes_accessed=4_000_000, transcendentals=0),
        name="row_inverse",
    )(z, table, order)


def turn(first, second, modulus):
    angle = ((first * second) % modulus).astype(F32) * (TWO_PI / modulus)
    return jnp.stack([jnp.cos(angle), jnp.sin(angle)])


def per_device(gate_out, gate_in, values, filter_spec, skip):
    col = lax.axis_index("col")
    low_side = col < 8
    table = jnp.asarray(row_table())

    order = jnp.asarray(place_moves())

    half = jnp.where(low_side, 0, 1).astype(jnp.int32)[None]
    other = filter_send(filter_spec, 1 - half)
    got = lax.ppermute(other, "col", [(i, 15 - i) for i in range(16)])

    gated = gate_in.astype(F32) * values.astype(F32)
    x = lax.all_to_all(gated.astype(BF16), "row", split_axis=0, concat_axis=0, tiled=True)

    extra_low = lax.ppermute(other[:, :, 0, :], "col", [(i, (16 - i) % 8) for i in range(8, 16)])
    extra_high = lax.ppermute(
        filter_spec[:, 2:, 0, :].astype(BF16), "col", [(i, 8 + (i - 1) % 8) for i in range(8, 16)]
    )
    extra = jnp.pad(jnp.where(low_side, extra_low, extra_high), ((0, 0), (0, 14), (0, 0)))
    moves = jnp.where(low_side, filter_moves()[0], filter_moves()[1])
    filt = filter_layout(filter_spec, half, got.reshape(2, 128, COLS), extra, moves)

    lane = jnp.arange(LANES, dtype=jnp.int32) % PER
    all_k1 = (PER * jnp.arange(BLOCKS, dtype=jnp.int32))[:, None, None] + lane[None, None, :]
    base = jnp.asarray(twist_base())
    phase = turn(all_k1, col, ROWS * 16)
    twist = jnp.stack(rotate(base[0], base[1], phase[0], phase[1]))
    y = row_forward(x.reshape(8, 4, 64, LANES), table, twist, order)
    y = lax.all_to_all(y, "col", split_axis=0, concat_axis=0, tiled=True)

    own_k1 = PER * jnp.where(low_side, col, 15 - col) + lane
    special = own_k1 == 0
    turn_k1 = jnp.where(special, -HALF, own_k1)
    within = turn(jnp.asarray(place_order(), jnp.int32)[:, None], turn_k1[None, :], TOTAL)[:, None]
    between = turn(jnp.arange(16, dtype=jnp.int32)[:, None, None], turn_k1[None, None, :], ROWS * 16)
    turns = jnp.stack(rotate(within[0], within[1], between[0], between[1]))
    z = column_step(
        y, turns, filt, jnp.asarray(step_tables()), jnp.asarray(middle_tables()), special.astype(F32)[None, :]
    )
    z = lax.all_to_all(z, "col", split_axis=0, concat_axis=0, tiled=True)

    convolved = row_inverse(z, table, order).reshape(32, 64, LANES)
    convolved = lax.all_to_all(convolved, "row", split_axis=0, concat_axis=0, tiled=True)
    return gate_out.astype(F32) * (convolved.astype(F32) + skip[:, None, None] * gated)


def solution(mesh):
    return jax.shard_map(
        per_device,
        mesh=mesh,
        in_specs=(
            P(None, "row", "col"),
            P(None, "row", "col"),
            P(None, "row", "col"),
            P(None, "row", "col", None),
            P(),
        ),
        out_specs=P(None, "row", "col"),
        check_vma=False,
    )
```

```python
import functools
import math

import jax
import jax.numpy as jnp
import ml_dtypes
import numpy as np
from jax import lax
from jax.experimental import pallas as pl
from jax.experimental.pallas import tpu as pltpu
from jax.sharding import PartitionSpec as P

ROWS = 1024
COLS = 2048
OUTER = 64
INNER = 32
HALF = ROWS // 2
TOTAL = ROWS * COLS
LANES = 128
BLOCKS = 8
PER = HALF // BLOCKS
TWO_PI = 2.0 * math.pi
BF16 = jnp.bfloat16
F32 = jnp.float32


def grid_angle(first, second, modulus):
    product = (np.asarray(first, np.int64)[:, None] * np.asarray(second, np.int64)[None, :]) % modulus
    return product.astype(np.float32) * np.float32(TWO_PI / modulus)


def narrow(array):
    return np.asarray(array, np.float32).astype(ml_dtypes.bfloat16)


def row_table():
    angle = grid_angle(np.arange(HALF), np.arange(HALF), ROWS)
    cosines, sines = np.cos(angle), -np.sin(angle)
    sines[:, 0] = 1.0 - 2.0 * (np.arange(HALF) % 2)
    parts = np.stack([cosines, sines], 0).reshape(2, HALF, BLOCKS, PER).transpose(1, 2, 0, 3)
    return narrow(np.repeat(parts[:, :, :, None, :], 2, 3).reshape(HALF, BLOCKS * 2 * 2 * PER))


def pair_order(table, first, second):
    rows, cols = table.shape[0] // 2, table.shape[1] // 2
    out = np.zeros((2, rows // first, 2, first, 2, cols // second, 2, second), np.float32)
    for which in range(2):
        out[:, :, which, :, :, :, which, :] = table.reshape(2, rows // first, first, 2, cols // second, second)
    return out.reshape(4 * rows, 4 * cols)


def outer_tables():
    near = grid_angle(np.arange(OUTER), np.arange(OUTER), OUTER)
    far = grid_angle(np.arange(OUTER) + 1, np.arange(OUTER), OUTER)
    c, s, cm, sm = np.cos(near), np.sin(near), np.cos(far), np.sin(far)
    return [
        pair_order(np.block([[c, s], [-s, c]]), 1, 4),
        pair_order(np.block([[cm, -sm], [-sm, -cm]]), 1, 4),
        pair_order(np.block([[c.T, -s.T], [s.T, c.T]]), 4, 1),
        pair_order(np.block([[cm.T, -sm.T], [-sm.T, -cm.T]]), 4, 1),
    ]


def inner_tables():
    angle = grid_angle(np.arange(INNER), np.arange(INNER), INNER)
    c, s = np.cos(angle), np.sin(angle)
    spread = np.zeros((2, 4, INNER, 2, INNER // 2, 4, 2), np.float32)
    for k in range(4):
        spread[:, k, :, :, :, k, :] = np.block([[c, s], [-s, c]]).reshape(2, INNER, 2, INNER // 2, 2)
    spread = spread.reshape(256, 256)
    return [spread, spread.T]


def step_tables():
    return narrow(np.stack(outer_tables() + inner_tables()))


def middle_tables():
    angle = grid_angle(np.arange(OUTER + 1), np.arange(INNER), COLS)
    sides = []
    for side in range(2):
        own = angle[side : side + OUTER].reshape(16, 4, 16, 2).transpose(0, 2, 1, 3).reshape(COLS, 1)
        own = np.pad(own.reshape(16, LANES).T, ((0, 0), (0, LANES - 16)))
        sides.append(np.stack([np.cos(own), np.sin(own)]))
    return np.stack(sides).astype(np.float32)


def place_order():
    return np.arange(LANES).reshape(4, INNER).T.reshape(-1)


def place_moves():
    return narrow(np.eye(LANES)[place_order()])


def twist_base():
    angle = grid_angle(place_order(), np.arange(PER), TOTAL)
    steps = np.pad(grid_angle(place_order(), PER * np.arange(BLOCKS), TOTAL), ((0, 0), (0, LANES - BLOCKS)))
    own = np.concatenate([np.cos(angle), np.sin(angle)], 1)
    return np.stack([own, np.cos(steps), np.sin(steps)]).astype(np.float32)


def filter_moves():
    moves = np.zeros((2, 2, 272, 256), np.float32)
    for copy in range(2):
        for e in range(PER):
            here, there, lane = copy * PER + e, copy * PER + (PER - e) % PER, copy * PER + e
            moves[0, :, here, lane] = 1.0
            moves[1, :, there, LANES + lane] = 1.0
            if e > 0:
                moves[0, :, LANES + there, LANES + lane] = 1.0
                moves[1, :, LANES + here, lane] = 1.0
            else:
                for part in range(2):
                    moves[0, part, 256 + 2 * part + copy, LANES + lane] = 1.0
                    moves[1, part, 256 + 2 * part + copy, lane] = 1.0
    return narrow(moves)


def rotate(real, imag, cosine, sine):
    return real * cosine - imag * sine, imag * cosine + real * sine


def filter_send_body(part, *refs):
    if part == 0:
        half_ref, spec_hbm, send_hbm, rows_ref, wide_ref, narrow_ref, in_sems, out_sems, lead_ref = refs
    else:
        half_ref, spec_hbm, ahead_ref, send_hbm, wide_ref, narrow_ref, in_sems, out_sems = refs
    away = 2 * (1 - half_ref[0])
    loads, stores = [], []

    def load(source, target):
        loads.append(pltpu.make_async_copy(source, target, in_sems.at[len(loads)]))
        loads[-1].start()

    for chan in range(2):
        for cut in range(2):
            rows = pl.ds(cut * 32, 32)
            load(spec_hbm.at[part, away + chan, rows], wide_ref.at[chan, rows])
            stores.append(
                pltpu.make_async_copy(
                    narrow_ref.at[chan, rows], send_hbm.at[chan, rows], out_sems.at[2 * chan + cut]
                )
            )
    if part == 0:
        for chan in range(2):
            load(spec_hbm.at[1, away + chan, pl.ds(0, 8)], lead_ref.at[chan])
    for chan in range(2):
        for cut in range(2):
            rows = pl.ds(cut * 32, 32)
            loads[2 * chan + cut].wait()
            narrow_ref[chan, rows] = wide_ref[chan, rows].astype(BF16)
            stores[2 * chan + cut].start()
    if part == 0:
        for copy in loads[4:]:
            copy.wait()
        firsts = [wide_ref[chan, 0:1, :] for chan in range(2)] + [lead_ref[chan, 0:1, :] for chan in range(2)]
        rows_ref[...] = jnp.concatenate(firsts + [jnp.zeros((12, COLS), F32)], 0).astype(BF16)
    for copy in stores:
        copy.wait()


def filter_send(part, spec, half, ahead=None):
    anywhere = pl.BlockSpec(memory_space=pl.ANY)
    first = part == 0
    return pl.pallas_call(
        functools.partial(filter_send_body, part),
        in_specs=[pl.BlockSpec(memory_space=pltpu.SMEM), anywhere] + ([] if first else [anywhere]),
        out_specs=[anywhere] + ([pl.BlockSpec(memory_space=pltpu.VMEM)] if first else []),
        out_shape=[jax.ShapeDtypeStruct((2, PER, COLS), BF16)]
        + ([jax.ShapeDtypeStruct((16, COLS), BF16)] if first else []),
        scratch_shapes=[
            pltpu.VMEM((2, PER, COLS), F32),
            pltpu.VMEM((2, PER, COLS), BF16),
            pltpu.SemaphoreType.DMA((6,)),
            pltpu.SemaphoreType.DMA((4,)),
        ]
        + ([pltpu.VMEM((2, 8, COLS), F32)] if first else []),
        compiler_params=pltpu.CompilerParams(vmem_limit_bytes=61 * 1024 * 1024),
        cost_estimate=pl.CostEstimate(flops=0, bytes_accessed=1_700_000, transcendentals=0),
        name="filter_send",
    )(*([half, spec] if first else [half, spec, ahead]))


def row_forward_body(
    x_hbm, table_ref, base_ref, phase_ref, order_ref, out_ref, x_ref, turned_ref, sems,
):
    copies = []

    def fetch(source, target):
        copies.append(pltpu.make_async_copy(source, target, sems.at[len(copies)]))
        copies[-1].start()
        return copies[-1]

    x_copies = [fetch(x_hbm.at[:, chan], x_ref.at[chan]) for chan in range(4)]
    for chan in range(4):
        x_copies[chan].wait()
        turned_ref[chan * LANES : (chan + 1) * LANES, :] = lax.dot_general(
            order_ref[...],
            x_ref[chan].reshape(HALF, LANES),
            (((1,), (1,)), ((), ())),
            preferred_element_type=F32,
        ).astype(BF16)

    lane = lax.broadcasted_iota(jnp.int32, (LANES, LANES), 1)
    first = lane < PER
    lead = lane % PER == 0
    base = base_ref[0]
    turned = pltpu.roll(base, PER, 1)
    own = jnp.where(first, base, turned), jnp.where(first, turned, base)

    def emit(place, real, imag):
        out_ref[place, 0] = real.astype(BF16)
        out_ref[place, 1] = imag.astype(BF16)

    high = []
    for block in range(BLOCKS):
        sums = jnp.dot(
            turned_ref[...], table_ref[:, block * 256 : (block + 1) * 256], preferred_element_type=F32
        )
        cosine, sine = rotate(
            *own, base_ref[1, :, block : block + 1], base_ref[2, :, block : block + 1]
        )
        cosine, sine = rotate(cosine, sine, phase_ref[0, block], phase_ref[1, block])
        for pair in range(2):
            upper = sums[pair * 256 : pair * 256 + 128]
            lower = sums[pair * 256 + 128 : pair * 256 + 256]
            real = jnp.where(first, upper[:, :LANES], lower[:, :LANES])
            imag = jnp.where(first, upper[:, LANES:], lower[:, LANES:])
            real, imag = rotate(real, imag, cosine, -sine)
            if pair == 0:
                emit(block, real, imag)
            else:
                high.append((real, imag))
        if block > 0:
            emit(16 - block, *(jnp.where(lead, new, old) for new, old in zip(high[block], high[block - 1])))
    emit(8, *(jnp.where(lead, new, old) for new, old in zip(high[0], high[7])))


def row_forward(x, table, base, phase, order):
    anywhere = pl.BlockSpec(memory_space=pl.ANY)
    inside = pl.BlockSpec(memory_space=pltpu.VMEM)
    block = (16, 2, LANES, LANES)
    return pl.pallas_call(
        row_forward_body,
        in_specs=[anywhere, inside, inside, inside, inside],
        out_specs=inside,
        out_shape=jax.ShapeDtypeStruct(block, BF16),
        scratch_shapes=[
            pltpu.VMEM((4, 8, 64, LANES), BF16),
            pltpu.VMEM((4 * LANES, HALF), BF16),
            pltpu.SemaphoreType.DMA((4,)),
        ],
        compiler_params=pltpu.CompilerParams(vmem_limit_bytes=16 * 1024 * 1024),
        cost_estimate=pl.CostEstimate(flops=1_100_000_000, bytes_accessed=5_000_000, transcendentals=0),
        name="row_forward",
    )(x, table, base, phase, order)


def filter_body(half_ref, own_ref, early_ref, late_ref, extra_ref, moves_ref, out_ref):
    for part in range(2):
        own = own_ref[part].reshape(LANES, own_ref.shape[3]).astype(BF16)
        got = (early_ref, late_ref)[part][...].reshape(LANES, early_ref.shape[2])
        total = None
        for source, low, high in ((own, 0, 128), (got, 128, 256), (extra_ref[...], 256, 272)):
            term = lax.dot_general(
                source, moves_ref[part, low:high, :], (((0,), (0,)), ((), ())), preferred_element_type=F32
            )
            total = term if total is None else total + term
        out_ref[0, part] = total[:, :LANES].astype(BF16)
        out_ref[1, part] = total[:, LANES:].astype(BF16)


def filter_layout(spec, half, early, late, extra, moves):
    step = 512
    return pl.pallas_call(
        filter_body,
        grid_spec=pltpu.PrefetchScalarGridSpec(
            num_scalar_prefetch=1,
            grid=(COLS // step,),
            in_specs=[
                pl.BlockSpec((2, 2, PER, step), lambda i, half: (0, half[0], 0, i)),
                pl.BlockSpec((2, PER, step), lambda i, half: (0, 0, i)),
                pl.BlockSpec((2, PER, step), lambda i, half: (0, 0, i)),
                pl.BlockSpec((16, step), lambda i, half: (0, i)),
                pl.BlockSpec((2, 272, 256), lambda i, half: (0, 0, 0)),
            ],
            out_specs=pl.BlockSpec((2, 2, step, LANES), lambda i, half: (0, 0, i, 0)),
        ),
        out_shape=jax.ShapeDtypeStruct((2, 2, COLS, LANES), BF16),
        compiler_params=pltpu.CompilerParams(vmem_limit_bytes=61 * 1024 * 1024),
        cost_estimate=pl.CostEstimate(flops=600_000_000, bytes_accessed=5_000_000, transcendentals=0),
        name="filter_layout",
    )(half, spec, early, late, extra, moves)


def column_body(
    y_hbm, filt_hbm, step_hbm, mid_ref, within_ref, between_ref, special_ref, out_ref,
    y_ref, turn_ref, filt_ref, step_ref, work_ref, sems,
):
    copies = []

    def fetch(source, target):
        copies.append(pltpu.make_async_copy(source, target, sems.at[len(copies)]))
        copies[-1].start()
        return copies[-1]

    y_copies = [fetch(y_hbm.at[pl.ds(8 * part, 8)], y_ref.at[pl.ds(8 * part, 8)]) for part in range(2)]
    step_copy = fetch(step_hbm.at[pl.ds(0, 2)], step_ref.at[pl.ds(0, 2)])
    later_copy = fetch(step_hbm.at[pl.ds(2, 4)], step_ref.at[pl.ds(2, 4)])
    filt_copies = []
    for part in range(4):
        rows = pl.ds(part * 512, 512)
        filt_copies.append(fetch(filt_hbm.at[:, :, rows], filt_ref.at[:, :, rows]))

    special = special_ref[...] > 0.5
    for copy in y_copies:
        copy.wait()
    step_copy.wait()

    def outer_forward(step):
        rows = slice(step * 16, step * 16 + 16)
        parts = [[], [], [], []]
        for block in range(16):
            real = y_ref[block, 0, rows, :].astype(F32)
            imag = y_ref[block, 1, rows, :].astype(F32)
            cosine, sine = rotate(
                within_ref[0, rows, :],
                within_ref[1, rows, :],
                between_ref[0, block : block + 1, :],
                between_ref[1, block : block + 1, :],
            )
            turn_ref[0, block, rows, :] = cosine
            turn_ref[1, block, rows, :] = sine
            parts[0].append(real)
            parts[1].append(jnp.where(special, 0.0, imag))
            parts[2].append(jnp.where(special, imag * cosine, real))
            parts[3].append(jnp.where(special, imag * sine, imag))
        for side in range(2):
            data = [
                jnp.concatenate(
                    [x[half * 8 : half * 8 + 8] for x in parts[2 * side] + parts[2 * side + 1]], 0
                ).astype(BF16)
                for half in range(2)
            ]
            sums = jnp.dot(step_ref[side], jnp.concatenate(data, 1), preferred_element_type=F32)
            for part in range(2):
                for group in range(16):
                    for half in range(2):
                        at = group * LANES + step * 16 + half * 8
                        work_ref[2 * side + part, at : at + 8, :] = sums[
                            part * LANES + group * 8 : part * LANES + group * 8 + 8,
                            half * LANES : (half + 1) * LANES,
                        ]

    def inner_step(step):
        if step % 4 == 0:
            filt_copies[step // 4].wait()
        rows = slice(step * LANES, (step + 1) * LANES)
        mid = [[mid_ref[side, part, :, step : step + 1] for part in range(2)] for side in range(2)]
        sides = []
        for side in range(2):
            real, imag = rotate(
                work_ref[2 * side, rows, :], work_ref[2 * side + 1, rows, :], mid[side][0], -mid[side][1]
            )
            sides.append(jnp.concatenate([real.astype(BF16), imag.astype(BF16)], 0))
        spectrum = jnp.dot(step_ref[4], jnp.concatenate(sides, 1), preferred_element_type=F32)
        sides = []
        for side in range(2):
            lanes = slice(side * LANES, (side + 1) * LANES)
            real, imag = rotate(
                spectrum[:LANES, lanes],
                spectrum[LANES:, lanes],
                filt_ref[side, 0, rows, :].astype(F32),
                filt_ref[side, 1, rows, :].astype(F32),
            )
            sides.append(jnp.concatenate([real.astype(BF16), imag.astype(BF16)], 0))
        middle = jnp.dot(step_ref[5], jnp.concatenate(sides, 1), preferred_element_type=F32)
        for side in range(2):
            lanes = slice(side * LANES, (side + 1) * LANES)
            real, imag = rotate(middle[:LANES, lanes], middle[LANES:, lanes], mid[side][0], mid[side][1])
            work_ref[2 * side, rows, :] = real
            work_ref[2 * side + 1, rows, :] = imag

    def outer_inverse(step):
        rows = slice(step * 16, step * 16 + 16)
        sums = []
        for side in range(2):
            data = []
            for half in range(2):
                pieces = []
                for part in range(2):
                    for group in range(16):
                        at = group * LANES + step * 16 + half * 8
                        pieces.append(work_ref[2 * side + part, at : at + 8, :])
                data.append(jnp.concatenate(pieces, 0).astype(BF16))
            sums.append(jnp.dot(step_ref[2 + side], jnp.concatenate(data, 1), preferred_element_type=F32))
        near, far = sums
        for block in range(16):

            def both(sums, part):
                at = part * LANES + block * 8
                return jnp.concatenate([sums[at : at + 8, :LANES], sums[at : at + 8, LANES:]], 0)

            near_re, near_im, far_re, far_im = both(near, 0), both(near, 1), both(far, 0), both(far, 1)
            cosine, sine = turn_ref[0, block, rows, :], turn_ref[1, block, rows, :]
            total_re, total_im = near_re + far_re, near_im + far_im
            real = jnp.where(special, near_re, total_re * cosine - total_im * sine)
            imag = jnp.where(special, far_re, total_im) * cosine + jnp.where(special, far_im, total_re) * sine
            out_ref[block, 0, rows, :] = real.astype(BF16)
            out_ref[block, 1, rows, :] = imag.astype(BF16)

    for step in range(8):
        outer_forward(step)
    later_copy.wait()
    for step in range(16):
        inner_step(step)
    for step in range(8):
        outer_inverse(step)


def column_step(y, filt, steps, mid, within, between, special):
    anywhere = pl.BlockSpec(memory_space=pl.ANY)
    block = (16, 2, LANES, LANES)
    return pl.pallas_call(
        column_body,
        in_specs=[anywhere] * 3 + [pl.BlockSpec(memory_space=pltpu.VMEM)] * 4,
        out_specs=pl.BlockSpec(memory_space=pltpu.VMEM),
        out_shape=jax.ShapeDtypeStruct(block, BF16),
        scratch_shapes=[
            pltpu.VMEM(block, BF16),
            pltpu.VMEM((2, 16, LANES, LANES), F32),
            pltpu.VMEM((2, 2, COLS, LANES), BF16),
            pltpu.VMEM((6, 256, 256), BF16),
            pltpu.VMEM((4, COLS, LANES), F32),
            pltpu.SemaphoreType.DMA((8,)),
        ],
        compiler_params=pltpu.CompilerParams(vmem_limit_bytes=60 * 1024 * 1024),
        cost_estimate=pl.CostEstimate(flops=2_000_000_000, bytes_accessed=10_000_000, transcendentals=0),
        name="column_step",
    )(y, filt, steps, mid, within, between, special)


def row_inverse_body(z_ref, table_ref, order_ref, out_ref, split_ref):
    lane = lax.broadcasted_iota(jnp.int32, (LANES, LANES), 1)
    first = lane < PER
    lead = lane % PER == 0
    for pair in range(2):
        for block in range(BLOCKS):
            for part in range(2):
                if pair == 0:
                    values = z_ref[block, part]
                else:
                    values = jnp.where(lead, z_ref[16 - block if block else 8, part], z_ref[15 - block, part])
                lanes = slice((block * 2 + part) * LANES, (block * 2 + part + 1) * LANES)
                zero = jnp.zeros_like(values)
                split_ref[pair * 256 : pair * 256 + 128, lanes] = jnp.where(first, values, zero)
                split_ref[pair * 256 + 128 : pair * 256 + 256, lanes] = jnp.where(first, zero, values)
        sums = lax.dot_general(
            table_ref[...],
            split_ref[pair * 256 : (pair + 1) * 256, :],
            (((1,), (1,)), ((), ())),
            preferred_element_type=F32,
        ) * (1.0 / TOTAL)
        for copy in range(2):
            own = sums[:, copy * LANES : (copy + 1) * LANES].astype(BF16)
            own = jnp.dot(own, order_ref[...], preferred_element_type=F32).astype(BF16)
            for row in range(8):
                out_ref[row, 2 * pair + copy] = own[row * 64 : (row + 1) * 64]


def row_inverse(z, table, order):
    inside = pl.BlockSpec(memory_space=pltpu.VMEM)
    return pl.pallas_call(
        row_inverse_body,
        in_specs=[inside] * 3,
        out_specs=inside,
        out_shape=jax.ShapeDtypeStruct((8, 4, 64, LANES), BF16),
        scratch_shapes=[pltpu.VMEM((4 * LANES, COLS), BF16)],
        compiler_params=pltpu.CompilerParams(vmem_limit_bytes=16 * 1024 * 1024),
        cost_estimate=pl.CostEstimate(flops=1_100_000_000, bytes_accessed=4_000_000, transcendentals=0),
        name="row_inverse",
    )(z, table, order)


def turn(first, second, modulus):
    angle = ((first * second) % modulus).astype(F32) * (TWO_PI / modulus)
    return jnp.stack([jnp.cos(angle), jnp.sin(angle)])


def per_device(gate_out, gate_in, values, filter_spec, skip):
    col = lax.axis_index("col")
    low_side = col < 8
    table = jnp.asarray(row_table())

    order = jnp.asarray(place_moves())

    half = jnp.where(low_side, 0, 1).astype(jnp.int32)[None]
    mirror = [(i, 15 - i) for i in range(16)]
    early_half, first_rows = filter_send(0, filter_spec, half)
    early = lax.ppermute(early_half, "col", mirror)
    extra = lax.ppermute(first_rows, "col", [(i, 16 - i if i % 8 else 8 - i) for i in range(16)])
    early_half, gate_in = lax.optimization_barrier((early_half, gate_in))
    gated = gate_in.astype(F32) * values.astype(F32)
    gated = gated.astype(BF16)
    x = lax.all_to_all(gated, "row", split_axis=0, concat_axis=0, tiled=True)
    late = lax.ppermute(filter_send(1, filter_spec, half, gated)[0], "col", mirror)
    moves = jnp.where(low_side, filter_moves()[0], filter_moves()[1])
    filt = filter_layout(filter_spec, half, early, late, extra, moves)

    lane = jnp.arange(LANES, dtype=jnp.int32) % PER
    all_k1 = (PER * jnp.arange(BLOCKS, dtype=jnp.int32))[:, None, None] + lane[None, None, :]
    phase = turn(all_k1, col, ROWS * 16)
    y = row_forward(x.reshape(8, 4, 64, LANES), table, twist_base(), phase, order)
    y = lax.all_to_all(y, "col", split_axis=0, concat_axis=0, tiled=True)

    own_k1 = PER * jnp.where(low_side, col, jnp.where(lane == 0, (16 - col) % 8, 15 - col)) + lane
    special = own_k1 == 0
    turn_k1 = jnp.where(special, -HALF, own_k1)
    within = turn(jnp.asarray(place_order(), jnp.int32)[:, None], turn_k1[None, :], TOTAL)
    between = turn(jnp.arange(16, dtype=jnp.int32)[:, None], turn_k1[None, :], ROWS * 16)
    z = column_step(
        y,
        filt,
        jnp.asarray(step_tables()),
        jnp.asarray(middle_tables()),
        within,
        between,
        special.astype(F32)[None, :],
    )
    z = lax.all_to_all(z, "col", split_axis=0, concat_axis=0, tiled=True)

    convolved = row_inverse(z, table, order).reshape(32, 64, LANES)
    convolved = lax.all_to_all(convolved, "row", split_axis=0, concat_axis=0, tiled=True)
    gated = gate_in.astype(F32) * values.astype(F32)
    return gate_out.astype(F32) * (convolved.astype(F32) + skip[:, None, None] * gated)


def solution(mesh):
    return jax.shard_map(
        per_device,
        mesh=mesh,
        in_specs=(
            P(None, "row", "col"),
            P(None, "row", "col"),
            P(None, "row", "col"),
            P(None, "row", "col", None),
            P(),
        ),
        out_specs=P(None, "row", "col"),
        check_vma=False,
    )
```

```python
import functools
import math

import jax
import jax.numpy as jnp
import ml_dtypes
import numpy as np
from jax import lax
from jax.experimental import pallas as pl
from jax.experimental.pallas import tpu as pltpu
from jax.sharding import PartitionSpec as P

ROWS = 1024
COLS = 2048
OUTER = 64
INNER = 32
HALF = ROWS // 2
TOTAL = ROWS * COLS
LANES = 128
BLOCKS = 8
PER = HALF // BLOCKS
TWO_PI = 2.0 * math.pi
BF16 = jnp.bfloat16
F32 = jnp.float32


def grid_angle(first, second, modulus):
    product = (np.asarray(first, np.int64)[:, None] * np.asarray(second, np.int64)[None, :]) % modulus
    return product.astype(np.float32) * np.float32(TWO_PI / modulus)


def narrow(array):
    return np.asarray(array, np.float32).astype(ml_dtypes.bfloat16)


def row_table():
    angle = grid_angle(np.arange(HALF), np.arange(HALF), ROWS)
    cosines, sines = np.cos(angle), -np.sin(angle)
    sines[:, 0] = 1.0 - 2.0 * (np.arange(HALF) % 2)
    parts = np.stack([cosines, sines], 0).reshape(2, HALF, BLOCKS, PER).transpose(1, 2, 0, 3)
    return narrow(np.repeat(parts[:, :, :, None, :], 2, 3).reshape(HALF, BLOCKS * 2 * 2 * PER))


def pair_order(table, first, second):
    rows, cols = table.shape[0] // 2, table.shape[1] // 2
    out = np.zeros((2, rows // first, 2, first, 2, cols // second, 2, second), np.float32)
    for which in range(2):
        out[:, :, which, :, :, :, which, :] = table.reshape(2, rows // first, first, 2, cols // second, second)
    return out.reshape(4 * rows, 4 * cols)


def outer_tables():
    near = grid_angle(np.arange(OUTER), np.arange(OUTER), OUTER)
    far = grid_angle(np.arange(OUTER) + 1, np.arange(OUTER), OUTER)
    c, s, cm, sm = np.cos(near), np.sin(near), np.cos(far), np.sin(far)
    return [
        pair_order(np.block([[c, s], [-s, c]]), 1, 4),
        pair_order(np.block([[cm, -sm], [-sm, -cm]]), 1, 4),
        pair_order(np.block([[c.T, -s.T], [s.T, c.T]]), 4, 1),
        pair_order(np.block([[cm.T, -sm.T], [-sm.T, -cm.T]]), 4, 1),
    ]


def inner_tables():
    angle = grid_angle(np.arange(INNER), np.arange(INNER), INNER)
    c, s = np.cos(angle), np.sin(angle)
    spread = np.zeros((2, 4, INNER, 2, INNER // 2, 4, 2), np.float32)
    for k in range(4):
        spread[:, k, :, :, :, k, :] = np.block([[c, s], [-s, c]]).reshape(2, INNER, 2, INNER // 2, 2)
    spread = spread.reshape(256, 256)
    return [spread, spread.T]


def step_tables():
    return narrow(np.stack(outer_tables() + inner_tables()))


def middle_index():
    product = np.arange(OUTER + 1)[:, None] * np.arange(INNER)[None, :]
    sides = []
    for side in range(2):
        own = product[side : side + OUTER].reshape(16, 4, 16, 2).transpose(0, 2, 1, 3).reshape(16, LANES).T
        sides.append(np.pad(own, ((0, 0), (0, LANES - 16))))
    return np.stack(sides).astype(np.int32)


def place_order():
    return np.arange(LANES).reshape(4, INNER).T.reshape(-1)


def place_moves():
    return narrow(np.eye(LANES)[place_order()])


def twist_base():
    angle = grid_angle(place_order(), np.arange(PER), TOTAL)
    steps = np.pad(grid_angle(place_order(), PER * np.arange(BLOCKS), TOTAL), ((0, 0), (0, LANES - BLOCKS)))
    own = np.concatenate([np.cos(angle), np.sin(angle)], 1)
    return np.stack([own, np.cos(steps), np.sin(steps)]).astype(np.float32)


def filter_moves():
    moves = np.zeros((2, 2, 272, 256), np.float32)
    for copy in range(2):
        for e in range(PER):
            here, there, lane = copy * PER + e, copy * PER + (PER - e) % PER, copy * PER + e
            moves[0, :, here, lane] = 1.0
            moves[1, :, there, LANES + lane] = 1.0
            if e > 0:
                moves[0, :, LANES + there, LANES + lane] = 1.0
                moves[1, :, LANES + here, lane] = 1.0
            else:
                for part in range(2):
                    moves[0, part, 256 + 2 * part + copy, LANES + lane] = 1.0
                    moves[1, part, 256 + 2 * part + copy, lane] = 1.0
    return narrow(moves)


def rotate(real, imag, cosine, sine):
    return real * cosine - imag * sine, imag * cosine + real * sine


def filter_send_body(part, *refs):
    if part == 0:
        half_ref, spec_hbm, send_hbm, rows_ref, wide_ref, narrow_ref, in_sems, out_sems, lead_ref = refs
    else:
        half_ref, spec_hbm, ahead_ref, send_hbm, wide_ref, narrow_ref, in_sems, out_sems = refs
    away = 2 * (1 - half_ref[0])
    loads, stores = [], []

    def load(source, target):
        loads.append(pltpu.make_async_copy(source, target, in_sems.at[len(loads)]))
        loads[-1].start()

    for chan in range(2):
        for cut in range(2):
            rows = pl.ds(cut * 32, 32)
            load(spec_hbm.at[part, away + chan, rows], wide_ref.at[chan, rows])
            stores.append(
                pltpu.make_async_copy(
                    narrow_ref.at[chan, rows], send_hbm.at[chan, rows], out_sems.at[2 * chan + cut]
                )
            )
    if part == 0:
        for chan in range(2):
            load(spec_hbm.at[1, away + chan, pl.ds(0, 8)], lead_ref.at[chan])
    for chan in range(2):
        for cut in range(2):
            rows = pl.ds(cut * 32, 32)
            loads[2 * chan + cut].wait()
            narrow_ref[chan, rows] = wide_ref[chan, rows].astype(BF16)
            stores[2 * chan + cut].start()
    if part == 0:
        for copy in loads[4:]:
            copy.wait()
        firsts = [wide_ref[chan, 0:1, :] for chan in range(2)] + [lead_ref[chan, 0:1, :] for chan in range(2)]
        rows_ref[...] = jnp.concatenate(firsts + [jnp.zeros((12, COLS), F32)], 0).astype(BF16)
    for copy in stores:
        copy.wait()


def filter_send(part, spec, half, ahead=None):
    anywhere = pl.BlockSpec(memory_space=pl.ANY)
    first = part == 0
    return pl.pallas_call(
        functools.partial(filter_send_body, part),
        in_specs=[pl.BlockSpec(memory_space=pltpu.SMEM), anywhere] + ([] if first else [anywhere]),
        out_specs=[anywhere] + ([pl.BlockSpec(memory_space=pltpu.VMEM)] if first else []),
        out_shape=[jax.ShapeDtypeStruct((2, PER, COLS), BF16)]
        + ([jax.ShapeDtypeStruct((16, COLS), BF16)] if first else []),
        scratch_shapes=[
            pltpu.VMEM((2, PER, COLS), F32),
            pltpu.VMEM((2, PER, COLS), BF16),
            pltpu.SemaphoreType.DMA((6,)),
            pltpu.SemaphoreType.DMA((4,)),
        ]
        + ([pltpu.VMEM((2, 8, COLS), F32)] if first else []),
        compiler_params=pltpu.CompilerParams(vmem_limit_bytes=61 * 1024 * 1024),
        cost_estimate=pl.CostEstimate(flops=0, bytes_accessed=1_700_000, transcendentals=0),
        name="filter_send",
    )(*([half, spec] if first else [half, spec, ahead]))


def row_forward_body(
    x_hbm, table_ref, base_ref, phase_ref, order_ref, out_ref, x_ref, turned_ref, sems,
):
    copies = []

    def fetch(source, target):
        copies.append(pltpu.make_async_copy(source, target, sems.at[len(copies)]))
        copies[-1].start()
        return copies[-1]

    x_copies = [fetch(x_hbm.at[:, chan], x_ref.at[chan]) for chan in range(4)]
    for chan in range(4):
        x_copies[chan].wait()
        turned_ref[chan * LANES : (chan + 1) * LANES, :] = lax.dot_general(
            order_ref[...],
            x_ref[chan].reshape(HALF, LANES),
            (((1,), (1,)), ((), ())),
            preferred_element_type=F32,
        ).astype(BF16)

    lane = lax.broadcasted_iota(jnp.int32, (LANES, LANES), 1)
    first = lane < PER
    lead = lane % PER == 0
    base = base_ref[0]
    turned = pltpu.roll(base, PER, 1)
    own = jnp.where(first, base, turned), jnp.where(first, turned, base)

    def emit(place, real, imag):
        out_ref[place, 0] = real.astype(BF16)
        out_ref[place, 1] = imag.astype(BF16)

    high = []
    for block in range(BLOCKS):
        sums = jnp.dot(
            turned_ref[...], table_ref[:, block * 256 : (block + 1) * 256], preferred_element_type=F32
        )
        cosine, sine = rotate(
            *own, base_ref[1, :, block : block + 1], base_ref[2, :, block : block + 1]
        )
        cosine, sine = rotate(cosine, sine, phase_ref[0, block], phase_ref[1, block])
        for pair in range(2):
            upper = sums[pair * 256 : pair * 256 + 128]
            lower = sums[pair * 256 + 128 : pair * 256 + 256]
            real = jnp.where(first, upper[:, :LANES], lower[:, :LANES])
            imag = jnp.where(first, upper[:, LANES:], lower[:, LANES:])
            real, imag = rotate(real, imag, cosine, -sine)
            if pair == 0:
                emit(block, real, imag)
            else:
                high.append((real, imag))
        if block > 0:
            emit(16 - block, *(jnp.where(lead, new, old) for new, old in zip(high[block], high[block - 1])))
    emit(8, *(jnp.where(lead, new, old) for new, old in zip(high[0], high[7])))


def row_forward(x, table, base, phase, order):
    anywhere = pl.BlockSpec(memory_space=pl.ANY)
    inside = pl.BlockSpec(memory_space=pltpu.VMEM)
    block = (16, 2, LANES, LANES)
    return pl.pallas_call(
        row_forward_body,
        in_specs=[anywhere, inside, inside, inside, inside],
        out_specs=inside,
        out_shape=jax.ShapeDtypeStruct(block, BF16),
        scratch_shapes=[
            pltpu.VMEM((4, 8, 64, LANES), BF16),
            pltpu.VMEM((4 * LANES, HALF), BF16),
            pltpu.SemaphoreType.DMA((4,)),
        ],
        compiler_params=pltpu.CompilerParams(vmem_limit_bytes=16 * 1024 * 1024),
        cost_estimate=pl.CostEstimate(flops=1_100_000_000, bytes_accessed=5_000_000, transcendentals=0),
        name="row_forward",
    )(x, table, base, phase, order)


def filter_body(half_ref, own_ref, early_ref, late_ref, extra_ref, moves_ref, out_ref):
    for part in range(2):
        own = own_ref[part].reshape(LANES, own_ref.shape[3]).astype(BF16)
        got = (early_ref, late_ref)[part][...].reshape(LANES, early_ref.shape[2])
        total = None
        for source, low, high in ((own, 0, 128), (got, 128, 256), (extra_ref[...], 256, 272)):
            term = lax.dot_general(
                source, moves_ref[part, low:high, :], (((0,), (0,)), ((), ())), preferred_element_type=F32
            )
            total = term if total is None else total + term
        out_ref[0, part] = total[:, :LANES].astype(BF16)
        out_ref[1, part] = total[:, LANES:].astype(BF16)


def filter_layout(spec, half, early, late, extra, moves):
    step = 512
    return pl.pallas_call(
        filter_body,
        grid_spec=pltpu.PrefetchScalarGridSpec(
            num_scalar_prefetch=1,
            grid=(COLS // step,),
            in_specs=[
                pl.BlockSpec((2, 2, PER, step), lambda i, half: (0, half[0], 0, i)),
                pl.BlockSpec((2, PER, step), lambda i, half: (0, 0, i)),
                pl.BlockSpec((2, PER, step), lambda i, half: (0, 0, i)),
                pl.BlockSpec((16, step), lambda i, half: (0, i)),
                pl.BlockSpec((2, 272, 256), lambda i, half: (0, 0, 0)),
            ],
            out_specs=pl.BlockSpec((2, 2, step, LANES), lambda i, half: (0, 0, i, 0)),
        ),
        out_shape=jax.ShapeDtypeStruct((2, 2, COLS, LANES), BF16),
        compiler_params=pltpu.CompilerParams(vmem_limit_bytes=55 * 1024 * 1024),
        cost_estimate=pl.CostEstimate(flops=600_000_000, bytes_accessed=5_000_000, transcendentals=0),
        name="filter_layout",
    )(half, spec, early, late, extra, moves)


def column_body(
    y_ref, filt_ref, step_ref, mid_ref, within_ref, between_ref, special_ref, out_ref, turn_ref, work_ref,
):
    special = special_ref[...] > 0.5

    def outer_forward(step):
        rows = slice(step * 16, step * 16 + 16)
        parts = [[], [], [], []]
        for block in range(16):
            real = y_ref[block, 0, rows, :].astype(F32)
            imag = y_ref[block, 1, rows, :].astype(F32)
            cosine, sine = rotate(
                within_ref[0, rows, :],
                within_ref[1, rows, :],
                between_ref[0, block : block + 1, :],
                between_ref[1, block : block + 1, :],
            )
            turn_ref[0, block, rows, :] = cosine
            turn_ref[1, block, rows, :] = sine
            parts[0].append(real)
            parts[1].append(jnp.where(special, 0.0, imag))
            parts[2].append(jnp.where(special, imag * cosine, real))
            parts[3].append(jnp.where(special, imag * sine, imag))
        for side in range(2):
            data = [
                jnp.concatenate(
                    [x[half * 8 : half * 8 + 8] for x in parts[2 * side] + parts[2 * side + 1]], 0
                ).astype(BF16)
                for half in range(2)
            ]
            sums = jnp.dot(step_ref[side], jnp.concatenate(data, 1), preferred_element_type=F32)
            for part in range(2):
                for group in range(16):
                    for half in range(2):
                        at = group * LANES + step * 16 + half * 8
                        work_ref[2 * side + part, at : at + 8, :] = sums[
                            part * LANES + group * 8 : part * LANES + group * 8 + 8,
                            half * LANES : (half + 1) * LANES,
                        ]

    def inner_step(step):
        rows = slice(step * LANES, (step + 1) * LANES)
        mid = [[mid_ref[part, side, :, step : step + 1] for part in range(2)] for side in range(2)]
        sides = []
        for side in range(2):
            real, imag = rotate(
                work_ref[2 * side, rows, :], work_ref[2 * side + 1, rows, :], mid[side][0], -mid[side][1]
            )
            sides.append(jnp.concatenate([real.astype(BF16), imag.astype(BF16)], 0))
        spectrum = jnp.dot(step_ref[4], jnp.concatenate(sides, 1), preferred_element_type=F32)
        sides = []
        for side in range(2):
            lanes = slice(side * LANES, (side + 1) * LANES)
            real, imag = rotate(
                spectrum[:LANES, lanes],
                spectrum[LANES:, lanes],
                filt_ref[side, 0, rows, :].astype(F32),
                filt_ref[side, 1, rows, :].astype(F32),
            )
            sides.append(jnp.concatenate([real.astype(BF16), imag.astype(BF16)], 0))
        middle = jnp.dot(step_ref[5], jnp.concatenate(sides, 1), preferred_element_type=F32)
        for side in range(2):
            lanes = slice(side * LANES, (side + 1) * LANES)
            real, imag = rotate(middle[:LANES, lanes], middle[LANES:, lanes], mid[side][0], mid[side][1])
            work_ref[2 * side, rows, :] = real
            work_ref[2 * side + 1, rows, :] = imag

    def outer_inverse(step):
        rows = slice(step * 16, step * 16 + 16)
        sums = []
        for side in range(2):
            data = []
            for half in range(2):
                pieces = []
                for part in range(2):
                    for group in range(16):
                        at = group * LANES + step * 16 + half * 8
                        pieces.append(work_ref[2 * side + part, at : at + 8, :])
                data.append(jnp.concatenate(pieces, 0).astype(BF16))
            sums.append(jnp.dot(step_ref[2 + side], jnp.concatenate(data, 1), preferred_element_type=F32))
        near, far = sums
        for block in range(16):

            def both(sums, part):
                at = part * LANES + block * 8
                return jnp.concatenate([sums[at : at + 8, :LANES], sums[at : at + 8, LANES:]], 0)

            near_re, near_im, far_re, far_im = both(near, 0), both(near, 1), both(far, 0), both(far, 1)
            cosine, sine = turn_ref[0, block, rows, :], turn_ref[1, block, rows, :]
            total_re, total_im = near_re + far_re, near_im + far_im
            real = jnp.where(special, near_re, total_re * cosine - total_im * sine)
            imag = jnp.where(special, far_re, total_im) * cosine + jnp.where(special, far_im, total_re) * sine
            out_ref[block, 0, rows, :] = real.astype(BF16)
            out_ref[block, 1, rows, :] = imag.astype(BF16)

    for step in range(8):
        outer_forward(step)
    for step in range(16):
        inner_step(step)
    for step in range(8):
        outer_inverse(step)


def column_step(y, filt, steps, mid, within, between, special):
    inside = pl.BlockSpec(memory_space=pltpu.VMEM)
    return pl.pallas_call(
        column_body,
        in_specs=[inside] * 7,
        out_specs=inside,
        out_shape=jax.ShapeDtypeStruct((16, 2, LANES, LANES), BF16),
        scratch_shapes=[pltpu.VMEM((2, 16, LANES, LANES), F32), pltpu.VMEM((4, COLS, LANES), F32)],
        compiler_params=pltpu.CompilerParams(vmem_limit_bytes=24 * 1024 * 1024),
        cost_estimate=pl.CostEstimate(flops=2_000_000_000, bytes_accessed=5_000_000, transcendentals=0),
        name="column_step",
    )(y, filt, steps, mid, within, between, special)


def row_inverse_body(z_ref, table_ref, order_ref, out_ref, split_ref):
    lane = lax.broadcasted_iota(jnp.int32, (LANES, LANES), 1)
    first = lane < PER
    lead = lane % PER == 0
    for pair in range(2):
        for block in range(BLOCKS):
            for part in range(2):
                if pair == 0:
                    values = z_ref[block, part]
                else:
                    values = jnp.where(lead, z_ref[16 - block if block else 8, part], z_ref[15 - block, part])
                lanes = slice((block * 2 + part) * LANES, (block * 2 + part + 1) * LANES)
                zero = jnp.zeros_like(values)
                split_ref[pair * 256 : pair * 256 + 128, lanes] = jnp.where(first, values, zero)
                split_ref[pair * 256 + 128 : pair * 256 + 256, lanes] = jnp.where(first, zero, values)
        sums = lax.dot_general(
            table_ref[...],
            split_ref[pair * 256 : (pair + 1) * 256, :],
            (((1,), (1,)), ((), ())),
            preferred_element_type=F32,
        ) * (1.0 / TOTAL)
        for copy in range(2):
            own = sums[:, copy * LANES : (copy + 1) * LANES].astype(BF16)
            own = jnp.dot(own, order_ref[...], preferred_element_type=F32).astype(BF16)
            for row in range(8):
                out_ref[row, 2 * pair + copy] = own[row * 64 : (row + 1) * 64]


def row_inverse(z, table, order):
    inside = pl.BlockSpec(memory_space=pltpu.VMEM)
    return pl.pallas_call(
        row_inverse_body,
        in_specs=[inside] * 3,
        out_specs=inside,
        out_shape=jax.ShapeDtypeStruct((8, 4, 64, LANES), BF16),
        scratch_shapes=[pltpu.VMEM((4 * LANES, COLS), BF16)],
        compiler_params=pltpu.CompilerParams(vmem_limit_bytes=16 * 1024 * 1024),
        cost_estimate=pl.CostEstimate(flops=1_100_000_000, bytes_accessed=4_000_000, transcendentals=0),
        name="row_inverse",
    )(z, table, order)


def turn(first, second, modulus):
    angle = ((first * second) % modulus).astype(F32) * (TWO_PI / modulus)
    return jnp.stack([jnp.cos(angle), jnp.sin(angle)])


def per_device(gate_out, gate_in, values, filter_spec, skip):
    col = lax.axis_index("col")
    low_side = col < 8
    table = jnp.asarray(row_table())

    order = jnp.asarray(place_moves())

    half = jnp.where(low_side, 0, 1).astype(jnp.int32)[None]
    mirror = [(i, 15 - i) for i in range(16)]
    early_half, first_rows = filter_send(0, filter_spec, half)
    early = lax.ppermute(early_half, "col", mirror)
    extra = lax.ppermute(first_rows, "col", [(i, 16 - i if i % 8 else 8 - i) for i in range(16)])
    early_half, gate_in = lax.optimization_barrier((early_half, gate_in))
    gated = gate_in.astype(F32) * values.astype(F32)
    gated = gated.astype(BF16)
    x = lax.all_to_all(gated, "row", split_axis=0, concat_axis=0, tiled=True)
    late = lax.ppermute(filter_send(1, filter_spec, half, gated)[0], "col", mirror)
    moves = jnp.where(low_side, filter_moves()[0], filter_moves()[1])
    filt = filter_layout(filter_spec, half, early, late, extra, moves)

    lane = jnp.arange(LANES, dtype=jnp.int32) % PER
    all_k1 = (PER * jnp.arange(BLOCKS, dtype=jnp.int32))[:, None, None] + lane[None, None, :]
    phase = turn(all_k1, col, ROWS * 16)
    y = row_forward(x.reshape(8, 4, 64, LANES), table, twist_base(), phase, order)
    y = lax.all_to_all(y, "col", split_axis=0, concat_axis=0, tiled=True)

    own_k1 = PER * jnp.where(low_side, col, jnp.where(lane == 0, (16 - col) % 8, 15 - col)) + lane
    special = own_k1 == 0
    turn_k1 = jnp.where(special, -HALF, own_k1)
    within = turn(jnp.asarray(place_order(), jnp.int32)[:, None], turn_k1[None, :], TOTAL)
    between = turn(jnp.arange(16, dtype=jnp.int32)[:, None], turn_k1[None, :], ROWS * 16)
    mid = turn(jnp.asarray(middle_index()), 1, COLS)
    steps = jnp.asarray(step_tables()) * (col >= 0).astype(BF16)
    z = column_step(y, filt, steps, mid, within, between, special.astype(F32)[None, :])
    z = lax.all_to_all(z, "col", split_axis=0, concat_axis=0, tiled=True)

    convolved = row_inverse(z, table, order).reshape(32, 64, LANES)
    convolved = lax.all_to_all(convolved, "row", split_axis=0, concat_axis=0, tiled=True)
    gated = gate_in.astype(F32) * values.astype(F32)
    return gate_out.astype(F32) * (convolved.astype(F32) + skip[:, None, None] * gated)


def solution(mesh):
    return jax.shard_map(
        per_device,
        mesh=mesh,
        in_specs=(
            P(None, "row", "col"),
            P(None, "row", "col"),
            P(None, "row", "col"),
            P(None, "row", "col", None),
            P(),
        ),
        out_specs=P(None, "row", "col"),
        check_vma=False,
    )
```

```python
import functools
import math

import jax
import jax.numpy as jnp
import ml_dtypes
import numpy as np
from jax import lax
from jax.experimental import pallas as pl
from jax.experimental.pallas import tpu as pltpu
from jax.sharding import PartitionSpec as P

ROWS = 1024
COLS = 2048
OUTER = 64
INNER = 32
HALF = ROWS // 2
TOTAL = ROWS * COLS
LANES = 128
BLOCKS = 8
PER = HALF // BLOCKS
TWO_PI = 2.0 * math.pi
BF16 = jnp.bfloat16
F32 = jnp.float32


def grid_angle(first, second, modulus):
    product = (np.asarray(first, np.int64)[:, None] * np.asarray(second, np.int64)[None, :]) % modulus
    return product.astype(np.float32) * np.float32(TWO_PI / modulus)


def narrow(array):
    return np.asarray(array, np.float32).astype(ml_dtypes.bfloat16)


def row_table():
    angle = grid_angle(np.arange(HALF), np.arange(HALF), ROWS)
    cosines, sines = np.cos(angle), -np.sin(angle)
    sines[:, 0] = 1.0 - 2.0 * (np.arange(HALF) % 2)
    parts = np.stack([cosines, sines], 0).reshape(2, HALF, BLOCKS, PER).transpose(1, 2, 0, 3)
    return narrow(np.repeat(parts[:, :, :, None, :], 2, 3).reshape(HALF, BLOCKS * 2 * 2 * PER))


def row_forward_table():
    both = row_table().reshape(HALF, BLOCKS, 2, 2, PER)
    return both[:, :, :, 0].reshape(HALF, BLOCKS * 2 * PER)


def pair_order(table, first, second):
    rows, cols = table.shape[0] // 2, table.shape[1] // 2
    out = np.zeros((2, rows // first, 2, first, 2, cols // second, 2, second), np.float32)
    for which in range(2):
        out[:, :, which, :, :, :, which, :] = table.reshape(2, rows // first, first, 2, cols // second, second)
    return out.reshape(4 * rows, 4 * cols)


def outer_tables():
    near = grid_angle(np.arange(OUTER), np.arange(OUTER), OUTER)
    far = grid_angle(np.arange(OUTER) + 1, np.arange(OUTER), OUTER)
    c, s, cm, sm = np.cos(near), np.sin(near), np.cos(far), np.sin(far)
    return [
        pair_order(np.block([[c, s], [-s, c]]), 1, 4),
        pair_order(np.block([[cm, -sm], [-sm, -cm]]), 1, 4),
        pair_order(np.block([[c.T, -s.T], [s.T, c.T]]), 4, 1),
        pair_order(np.block([[cm.T, -sm.T], [-sm.T, -cm.T]]), 4, 1),
    ]


def inner_tables():
    angle = grid_angle(np.arange(INNER), np.arange(INNER), INNER)
    c, s = np.cos(angle), np.sin(angle)
    spread = np.zeros((2, 4, INNER, 2, INNER // 2, 4, 2), np.float32)
    for k in range(4):
        spread[:, k, :, :, :, k, :] = np.block([[c, s], [-s, c]]).reshape(2, INNER, 2, INNER // 2, 2)
    spread = spread.reshape(256, 256)
    return [spread, spread.T]


def step_tables():
    return narrow(np.stack(outer_tables() + inner_tables()))


def middle_index():
    product = np.arange(OUTER + 1)[:, None] * np.arange(INNER)[None, :]
    sides = []
    for side in range(2):
        own = product[side : side + OUTER].reshape(16, 4, 16, 2).transpose(0, 2, 1, 3).reshape(16, LANES).T
        sides.append(np.pad(own, ((0, 0), (0, LANES - 16))))
    return np.stack(sides).astype(np.int32)


def place_order():
    return np.arange(LANES).reshape(4, INNER).T.reshape(-1)


def place_moves():
    return narrow(np.eye(LANES)[place_order()])


def twist_base():
    angle = grid_angle(place_order(), np.arange(PER), TOTAL)
    steps = np.pad(grid_angle(place_order(), PER * np.arange(BLOCKS), TOTAL), ((0, 0), (0, LANES - BLOCKS)))
    own = np.concatenate([np.cos(angle), np.sin(angle)], 1)
    return np.stack([own, np.cos(steps), np.sin(steps)]).astype(np.float32)


def filter_moves():
    moves = np.zeros((2, 2, 272, 256), np.float32)
    for copy in range(2):
        for e in range(PER):
            here, there, lane = copy * PER + e, copy * PER + (PER - e) % PER, copy * PER + e
            moves[0, :, here, lane] = 1.0
            moves[1, :, there, LANES + lane] = 1.0
            if e > 0:
                moves[0, :, LANES + there, LANES + lane] = 1.0
                moves[1, :, LANES + here, lane] = 1.0
            else:
                for part in range(2):
                    moves[0, part, 256 + 2 * part + copy, LANES + lane] = 1.0
                    moves[1, part, 256 + 2 * part + copy, lane] = 1.0
    return narrow(moves)


def rotate(real, imag, cosine, sine):
    return real * cosine - imag * sine, imag * cosine + real * sine


def filter_send_body(part, *refs):
    if part == 0:
        half_ref, spec_hbm, send_ref, rows_ref, wide_ref, in_sems, lead_ref = refs
    else:
        half_ref, spec_hbm, ahead_ref, send_hbm, wide_ref, in_sems, send_ref, out_sems = refs
    away = 2 * (1 - half_ref[0])
    loads, stores = [], []

    def load(source, target):
        loads.append(pltpu.make_async_copy(source, target, in_sems.at[len(loads)]))
        loads[-1].start()

    for chan in range(2):
        for cut in range(2):
            rows = pl.ds(cut * 32, 32)
            load(spec_hbm.at[part, away + chan, rows], wide_ref.at[chan, rows])
    if part == 0:
        for chan in range(2):
            load(spec_hbm.at[1, away + chan, pl.ds(0, 8)], lead_ref.at[chan])
    for chan in range(2):
        for cut in range(2):
            rows = pl.ds(cut * 32, 32)
            loads[2 * chan + cut].wait()
            send_ref[chan, rows] = wide_ref[chan, rows].astype(BF16)
            if part == 1:
                stores.append(
                    pltpu.make_async_copy(
                        send_ref.at[chan, rows], send_hbm.at[chan, rows], out_sems.at[2 * chan + cut]
                    )
                )
                stores[-1].start()
    if part == 0:
        for copy in loads[4:]:
            copy.wait()
        firsts = [wide_ref[chan, 0:1, :] for chan in range(2)] + [lead_ref[chan, 0:1, :] for chan in range(2)]
        rows_ref[...] = jnp.concatenate(firsts + [jnp.zeros((12, COLS), F32)], 0).astype(BF16)
    for copy in stores:
        copy.wait()


def filter_send(part, spec, half, ahead=None):
    anywhere = pl.BlockSpec(memory_space=pl.ANY)
    first = part == 0
    return pl.pallas_call(
        functools.partial(filter_send_body, part),
        in_specs=[pl.BlockSpec(memory_space=pltpu.SMEM), anywhere] + ([] if first else [anywhere]),
        out_specs=[pl.BlockSpec(memory_space=pltpu.VMEM)] * 2 if first else [anywhere],
        out_shape=[pltpu.VMEM((2, PER, COLS), BF16), jax.ShapeDtypeStruct((16, COLS), BF16)]
        if first
        else [jax.ShapeDtypeStruct((2, PER, COLS), BF16)],
        scratch_shapes=[
            pltpu.VMEM((2, PER, COLS), F32),
            pltpu.SemaphoreType.DMA((6,)),
        ]
        + (
            [pltpu.VMEM((2, 8, COLS), F32)]
            if first
            else [pltpu.VMEM((2, PER, COLS), BF16), pltpu.SemaphoreType.DMA((4,))]
        ),
        compiler_params=pltpu.CompilerParams(vmem_limit_bytes=(61 if first else 59) * 1024 * 1024),
        cost_estimate=pl.CostEstimate(flops=0, bytes_accessed=1_700_000, transcendentals=0),
        name="filter_send",
    )(*([half, spec] if first else [half, spec, ahead]))


def row_forward_body(
    x_ref, table_ref, base_ref, phase_ref, order_ref, out_ref, turned_ref,
):
    for chan in range(4):
        turned_ref[chan * LANES : (chan + 1) * LANES, :] = lax.dot_general(
            order_ref[...],
            x_ref[:, chan].reshape(HALF, LANES),
            (((1,), (1,)), ((), ())),
            preferred_element_type=F32,
        ).astype(BF16)

    lane = lax.broadcasted_iota(jnp.int32, (LANES, LANES), 1)
    first = lane < PER
    lead = lane % PER == 0
    base = base_ref[0]
    turned = pltpu.roll(base, PER, 1)
    own = jnp.where(first, base, turned), jnp.where(first, turned, base)

    def emit(place, real, imag):
        out_ref[place, 0] = real.astype(BF16)
        out_ref[place, 1] = imag.astype(BF16)

    high = []
    for block in range(BLOCKS):
        if block % 2 == 0:
            sums = jnp.dot(
                turned_ref[...], table_ref[:, block * LANES : (block + 2) * LANES], preferred_element_type=F32
            )
        cosine, sine = rotate(
            *own, base_ref[1, :, block : block + 1], base_ref[2, :, block : block + 1]
        )
        cosine, sine = rotate(cosine, sine, phase_ref[0, block], phase_ref[1, block])
        for pair in range(2):
            lanes = slice(block % 2 * LANES, block % 2 * LANES + LANES)
            upper = sums[pair * 256 : pair * 256 + 128, lanes]
            lower = sums[pair * 256 + 128 : pair * 256 + 256, lanes]
            real = jnp.where(first, upper, pltpu.roll(lower, PER, 1))
            imag = jnp.where(first, pltpu.roll(upper, PER, 1), lower)
            real, imag = rotate(real, imag, cosine, -sine)
            if pair == 0:
                emit(block, real, imag)
            else:
                high.append((real, imag))
        if block > 0:
            emit(16 - block, *(jnp.where(lead, new, old) for new, old in zip(high[block], high[block - 1])))
    emit(8, *(jnp.where(lead, new, old) for new, old in zip(high[0], high[7])))


def row_forward(x, table, base, phase, order):
    inside = pl.BlockSpec(memory_space=pltpu.VMEM)
    block = (16, 2, LANES, LANES)
    return pl.pallas_call(
        row_forward_body,
        in_specs=[inside] * 5,
        out_specs=inside,
        out_shape=jax.ShapeDtypeStruct(block, BF16),
        scratch_shapes=[
            pltpu.VMEM((4 * LANES, HALF), BF16),
        ],
        compiler_params=pltpu.CompilerParams(vmem_limit_bytes=16 * 1024 * 1024),
        cost_estimate=pl.CostEstimate(flops=1_100_000_000, bytes_accessed=5_000_000, transcendentals=0),
        name="row_forward",
    )(x, table, base, phase, order)


def filter_body(half_ref, own_ref, early_ref, late_ref, extra_ref, moves_ref, out_ref):
    for part in range(2):
        own = own_ref[part].reshape(LANES, own_ref.shape[3]).astype(BF16)
        got = (early_ref, late_ref)[part][...].reshape(LANES, early_ref.shape[2])
        total = None
        for source, low, high in ((own, 0, 128), (got, 128, 256), (extra_ref[...], 256, 272)):
            term = lax.dot_general(
                source, moves_ref[part, low:high, :], (((0,), (0,)), ((), ())), preferred_element_type=F32
            )
            total = term if total is None else total + term
        out_ref[0, part] = total[:, :LANES].astype(BF16)
        out_ref[1, part] = total[:, LANES:].astype(BF16)


def filter_layout(spec, half, early, late, extra, moves):
    step = 512
    return pl.pallas_call(
        filter_body,
        grid_spec=pltpu.PrefetchScalarGridSpec(
            num_scalar_prefetch=1,
            grid=(COLS // step,),
            in_specs=[
                pl.BlockSpec((2, 2, PER, step), lambda i, half: (0, half[0], 0, i)),
                pl.BlockSpec((2, PER, step), lambda i, half: (0, 0, i)),
                pl.BlockSpec((2, PER, step), lambda i, half: (0, 0, i)),
                pl.BlockSpec((16, step), lambda i, half: (0, i)),
                pl.BlockSpec((2, 272, 256), lambda i, half: (0, 0, 0)),
            ],
            out_specs=pl.BlockSpec((2, 2, step, LANES), lambda i, half: (0, 0, i, 0)),
        ),
        out_shape=jax.ShapeDtypeStruct((2, 2, COLS, LANES), BF16),
        compiler_params=pltpu.CompilerParams(vmem_limit_bytes=55 * 1024 * 1024),
        cost_estimate=pl.CostEstimate(flops=600_000_000, bytes_accessed=5_000_000, transcendentals=0),
        name="filter_layout",
    )(half, spec, early, late, extra, moves)


def column_body(
    y_ref, filt_ref, step_ref, mid_ref, within_ref, between_ref, special_ref, out_ref, turn_ref, work_ref,
):
    special = special_ref[...] > 0.5

    def outer_forward(step):
        rows = slice(step * 16, step * 16 + 16)
        parts = [[], [], [], []]
        for block in range(16):
            real = y_ref[block, 0, rows, :].astype(F32)
            imag = y_ref[block, 1, rows, :].astype(F32)
            cosine, sine = rotate(
                within_ref[0, rows, :],
                within_ref[1, rows, :],
                between_ref[0, block : block + 1, :],
                between_ref[1, block : block + 1, :],
            )
            turn_ref[0, block, rows, :] = cosine
            turn_ref[1, block, rows, :] = sine
            parts[0].append(real)
            parts[1].append(jnp.where(special, 0.0, imag))
            parts[2].append(jnp.where(special, imag * cosine, real))
            parts[3].append(jnp.where(special, imag * sine, imag))
        for side in range(2):
            data = [
                jnp.concatenate(
                    [x[half * 8 : half * 8 + 8] for x in parts[2 * side] + parts[2 * side + 1]], 0
                ).astype(BF16)
                for half in range(2)
            ]
            sums = jnp.dot(step_ref[side], jnp.concatenate(data, 1), preferred_element_type=F32)
            for part in range(2):
                for group in range(16):
                    for half in range(2):
                        at = group * LANES + step * 16 + half * 8
                        work_ref[2 * side + part, at : at + 8, :] = sums[
                            part * LANES + group * 8 : part * LANES + group * 8 + 8,
                            half * LANES : (half + 1) * LANES,
                        ]

    def inner_step(step):
        rows = slice(step * LANES, (step + 1) * LANES)
        mid = [[mid_ref[part, side, :, step : step + 1] for part in range(2)] for side in range(2)]
        sides = []
        for side in range(2):
            real, imag = rotate(
                work_ref[2 * side, rows, :], work_ref[2 * side + 1, rows, :], mid[side][0], -mid[side][1]
            )
            sides.append(jnp.concatenate([real.astype(BF16), imag.astype(BF16)], 0))
        spectrum = jnp.dot(step_ref[4], jnp.concatenate(sides, 1), preferred_element_type=F32)
        sides = []
        for side in range(2):
            lanes = slice(side * LANES, (side + 1) * LANES)
            real, imag = rotate(
                spectrum[:LANES, lanes],
                spectrum[LANES:, lanes],
                filt_ref[side, 0, rows, :].astype(F32),
                filt_ref[side, 1, rows, :].astype(F32),
            )
            sides.append(jnp.concatenate([real.astype(BF16), imag.astype(BF16)], 0))
        middle = jnp.dot(step_ref[5], jnp.concatenate(sides, 1), preferred_element_type=F32)
        for side in range(2):
            lanes = slice(side * LANES, (side + 1) * LANES)
            real, imag = rotate(middle[:LANES, lanes], middle[LANES:, lanes], mid[side][0], mid[side][1])
            work_ref[2 * side, rows, :] = real
            work_ref[2 * side + 1, rows, :] = imag

    def outer_inverse(step):
        rows = slice(step * 16, step * 16 + 16)
        sums = []
        for side in range(2):
            data = []
            for half in range(2):
                pieces = []
                for part in range(2):
                    for group in range(16):
                        at = group * LANES + step * 16 + half * 8
                        pieces.append(work_ref[2 * side + part, at : at + 8, :])
                data.append(jnp.concatenate(pieces, 0).astype(BF16))
            sums.append(jnp.dot(step_ref[2 + side], jnp.concatenate(data, 1), preferred_element_type=F32))
        near, far = sums
        for block in range(16):

            def both(sums, part):
                at = part * LANES + block * 8
                return jnp.concatenate([sums[at : at + 8, :LANES], sums[at : at + 8, LANES:]], 0)

            near_re, near_im, far_re, far_im = both(near, 0), both(near, 1), both(far, 0), both(far, 1)
            cosine, sine = turn_ref[0, block, rows, :], turn_ref[1, block, rows, :]
            total_re, total_im = near_re + far_re, near_im + far_im
            real = jnp.where(special, near_re, total_re * cosine - total_im * sine)
            imag = jnp.where(special, far_re, total_im) * cosine + jnp.where(special, far_im, total_re) * sine
            out_ref[block, 0, rows, :] = real.astype(BF16)
            out_ref[block, 1, rows, :] = imag.astype(BF16)

    for step in range(8):
        outer_forward(step)
    for step in range(16):
        inner_step(step)
    for step in range(8):
        outer_inverse(step)


def column_step(y, filt, steps, mid, within, between, special):
    inside = pl.BlockSpec(memory_space=pltpu.VMEM)
    return pl.pallas_call(
        column_body,
        in_specs=[inside] * 7,
        out_specs=inside,
        out_shape=jax.ShapeDtypeStruct((16, 2, LANES, LANES), BF16),
        scratch_shapes=[pltpu.VMEM((2, 16, LANES, LANES), F32), pltpu.VMEM((4, COLS, LANES), F32)],
        compiler_params=pltpu.CompilerParams(vmem_limit_bytes=24 * 1024 * 1024),
        cost_estimate=pl.CostEstimate(flops=2_000_000_000, bytes_accessed=5_000_000, transcendentals=0),
        name="column_step",
    )(y, filt, steps, mid, within, between, special)


def row_inverse_body(z_ref, table_ref, order_ref, out_ref, split_ref):
    lane = lax.broadcasted_iota(jnp.int32, (LANES, LANES), 1)
    first = lane < PER
    lead = lane % PER == 0
    for pair in range(2):
        for block in range(BLOCKS):
            for part in range(2):
                if pair == 0:
                    values = z_ref[block, part]
                else:
                    values = jnp.where(lead, z_ref[16 - block if block else 8, part], z_ref[15 - block, part])
                lanes = slice((block * 2 + part) * LANES, (block * 2 + part + 1) * LANES)
                zero = jnp.zeros_like(values)
                split_ref[pair * 256 : pair * 256 + 128, lanes] = jnp.where(first, values, zero)
                split_ref[pair * 256 + 128 : pair * 256 + 256, lanes] = jnp.where(first, zero, values)
        sums = lax.dot_general(
            table_ref[...],
            split_ref[pair * 256 : (pair + 1) * 256, :],
            (((1,), (1,)), ((), ())),
            preferred_element_type=F32,
        ) * (1.0 / TOTAL)
        for copy in range(2):
            own = sums[:, copy * LANES : (copy + 1) * LANES].astype(BF16)
            own = jnp.dot(own, order_ref[...], preferred_element_type=F32).astype(BF16)
            for row in range(8):
                out_ref[row, 2 * pair + copy] = own[row * 64 : (row + 1) * 64]


def row_inverse(z, table, order):
    inside = pl.BlockSpec(memory_space=pltpu.VMEM)
    return pl.pallas_call(
        row_inverse_body,
        in_specs=[inside] * 3,
        out_specs=inside,
        out_shape=jax.ShapeDtypeStruct((8, 4, 64, LANES), BF16),
        scratch_shapes=[pltpu.VMEM((4 * LANES, COLS), BF16)],
        compiler_params=pltpu.CompilerParams(vmem_limit_bytes=16 * 1024 * 1024),
        cost_estimate=pl.CostEstimate(flops=1_100_000_000, bytes_accessed=4_000_000, transcendentals=0),
        name="row_inverse",
    )(z, table, order)


def turn(first, second, modulus):
    angle = ((first * second) % modulus).astype(F32) * (TWO_PI / modulus)
    return jnp.stack([jnp.cos(angle), jnp.sin(angle)])


def per_device(gate_out, gate_in, values, filter_spec, skip):
    col = lax.axis_index("col")
    low_side = col < 8
    table = jnp.asarray(row_table())

    order = jnp.asarray(place_moves())

    half = jnp.where(low_side, 0, 1).astype(jnp.int32)[None]
    mirror = [(i, 15 - i) for i in range(16)]
    early_half, first_rows = filter_send(0, filter_spec, half)
    early = lax.ppermute(early_half, "col", mirror)
    extra = lax.ppermute(first_rows, "col", [(i, 16 - i if i % 8 else 8 - i) for i in range(16)])
    early_half, gate_in = lax.optimization_barrier((early_half, gate_in))
    gated = gate_in.astype(F32) * values.astype(F32)
    gated = gated.astype(BF16)
    x = lax.all_to_all(gated, "row", split_axis=0, concat_axis=0, tiled=True)
    late = lax.ppermute(filter_send(1, filter_spec, half, gated)[0], "col", mirror)
    moves = jnp.where(low_side, filter_moves()[0], filter_moves()[1])
    filt = filter_layout(filter_spec, half, early, late, extra, moves)

    lane = jnp.arange(LANES, dtype=jnp.int32) % PER
    all_k1 = (PER * jnp.arange(BLOCKS, dtype=jnp.int32))[:, None, None] + lane[None, None, :]
    phase = turn(all_k1, col, ROWS * 16)
    y = row_forward(x.reshape(8, 4, 64, LANES), jnp.asarray(row_forward_table()), twist_base(), phase, order)
    y = lax.all_to_all(y, "col", split_axis=0, concat_axis=0, tiled=True)

    own_k1 = PER * jnp.where(low_side, col, jnp.where(lane == 0, (16 - col) % 8, 15 - col)) + lane
    special = own_k1 == 0
    turn_k1 = jnp.where(special, -HALF, own_k1)
    within = turn(jnp.asarray(place_order(), jnp.int32)[:, None], turn_k1[None, :], TOTAL)
    between = turn(jnp.arange(16, dtype=jnp.int32)[:, None], turn_k1[None, :], ROWS * 16)
    mid = turn(jnp.asarray(middle_index()), 1, COLS)
    steps = jnp.asarray(step_tables()) * (col >= 0).astype(BF16)
    z = column_step(y, filt, steps, mid, within, between, special.astype(F32)[None, :])
    z = lax.all_to_all(z, "col", split_axis=0, concat_axis=0, tiled=True)

    convolved = row_inverse(z, table, order).reshape(32, 64, LANES)
    convolved = lax.all_to_all(convolved, "row", split_axis=0, concat_axis=0, tiled=True)
    gated = gate_in.astype(F32) * values.astype(F32)
    return gate_out.astype(F32) * (convolved.astype(F32) + skip[:, None, None] * gated)


def solution(mesh):
    return jax.shard_map(
        per_device,
        mesh=mesh,
        in_specs=(
            P(None, "row", "col"),
            P(None, "row", "col"),
            P(None, "row", "col"),
            P(None, "row", "col", None),
            P(),
        ),
        out_specs=P(None, "row", "col"),
        check_vma=False,
    )
```

```python
import functools
import math

import jax
import jax.numpy as jnp
import ml_dtypes
import numpy as np
from jax import lax
from jax.experimental import pallas as pl
from jax.experimental.pallas import tpu as pltpu
from jax.sharding import PartitionSpec as P

ROWS = 1024
COLS = 2048
OUTER = 64
INNER = 32
HALF = ROWS // 2
TOTAL = ROWS * COLS
LANES = 128
BLOCKS = 8
PER = HALF // BLOCKS
TWO_PI = 2.0 * math.pi
BF16 = jnp.bfloat16
F32 = jnp.float32


def grid_angle(first, second, modulus):
    product = (np.asarray(first, np.int64)[:, None] * np.asarray(second, np.int64)[None, :]) % modulus
    return product.astype(np.float32) * np.float32(TWO_PI / modulus)


def narrow(array):
    return np.asarray(array, np.float32).astype(ml_dtypes.bfloat16)


def row_table():
    angle = grid_angle(np.arange(HALF), np.arange(HALF), ROWS)
    cosines, sines = np.cos(angle), -np.sin(angle)
    sines[:, 0] = 1.0 - 2.0 * (np.arange(HALF) % 2)
    parts = np.stack([cosines, sines], 0).reshape(2, HALF, BLOCKS, PER).transpose(1, 2, 0, 3)
    return narrow(parts.reshape(HALF, BLOCKS * 2 * PER))


def pair_order(table, first, second):
    rows, cols = table.shape[0] // 2, table.shape[1] // 2
    out = np.zeros((2, rows // first, 2, first, 2, cols // second, 2, second), np.float32)
    for which in range(2):
        out[:, :, which, :, :, :, which, :] = table.reshape(2, rows // first, first, 2, cols // second, second)
    return out.reshape(4 * rows, 4 * cols)


def outer_tables():
    near = grid_angle(np.arange(OUTER), np.arange(OUTER), OUTER)
    far = grid_angle(np.arange(OUTER) + 1, np.arange(OUTER), OUTER)
    c, s, cm, sm = np.cos(near), np.sin(near), np.cos(far), np.sin(far)
    return [
        pair_order(np.block([[c, s], [-s, c]]), 1, 4),
        pair_order(np.block([[cm, -sm], [-sm, -cm]]), 1, 4),
        pair_order(np.block([[c.T, -s.T], [s.T, c.T]]), 4, 1),
        pair_order(np.block([[cm.T, -sm.T], [-sm.T, -cm.T]]), 4, 1),
    ]


def inner_tables():
    angle = grid_angle(np.arange(INNER), np.arange(INNER), INNER)
    c, s = np.cos(angle), np.sin(angle)
    spread = np.zeros((2, 4, INNER, 2, INNER // 2, 4, 2), np.float32)
    for k in range(4):
        spread[:, k, :, :, :, k, :] = np.block([[c, s], [-s, c]]).reshape(2, INNER, 2, INNER // 2, 2)
    spread = spread.reshape(256, 256)
    return [spread, spread.T]


def step_tables():
    return narrow(np.stack(outer_tables() + inner_tables()))


def middle_index():
    product = np.arange(OUTER + 1)[:, None] * np.arange(INNER)[None, :]
    sides = []
    for side in range(2):
        own = product[side : side + OUTER].reshape(16, 4, 16, 2).transpose(0, 2, 1, 3).reshape(16, LANES).T
        sides.append(np.pad(own, ((0, 0), (0, LANES - 16))))
    return np.stack(sides).astype(np.int32)


def place_order():
    return np.arange(LANES).reshape(4, INNER).T.reshape(-1)


def place_moves():
    return narrow(np.eye(LANES)[place_order()])


def twist_base():
    angle = grid_angle(place_order(), np.arange(PER), TOTAL)
    steps = np.pad(grid_angle(place_order(), PER * np.arange(BLOCKS), TOTAL), ((0, 0), (0, LANES - BLOCKS)))
    own = np.concatenate([np.cos(angle), np.sin(angle)], 1)
    return np.stack([own, np.cos(steps), np.sin(steps)]).astype(np.float32)


def filter_moves():
    moves = np.zeros((2, 2, 272, 256), np.float32)
    for copy in range(2):
        for e in range(PER):
            here, there, lane = copy * PER + e, copy * PER + (PER - e) % PER, copy * PER + e
            moves[0, :, here, lane] = 1.0
            moves[1, :, there, LANES + lane] = 1.0
            if e > 0:
                moves[0, :, LANES + there, LANES + lane] = 1.0
                moves[1, :, LANES + here, lane] = 1.0
            else:
                for part in range(2):
                    moves[0, part, 256 + 2 * part + copy, LANES + lane] = 1.0
                    moves[1, part, 256 + 2 * part + copy, lane] = 1.0
    return narrow(moves)


def rotate(real, imag, cosine, sine):
    return real * cosine - imag * sine, imag * cosine + real * sine


def filter_send_body(part, *refs):
    if part == 0:
        half_ref, spec_hbm, send_ref, rows_ref, wide_ref, in_sems, lead_ref = refs
    else:
        half_ref, spec_hbm, ahead_ref, send_hbm, wide_ref, in_sems, send_ref, out_sems = refs
    away = 2 * (1 - half_ref[0])
    loads, stores = [], []

    def load(source, target):
        loads.append(pltpu.make_async_copy(source, target, in_sems.at[len(loads)]))
        loads[-1].start()

    for chan in range(2):
        for cut in range(2):
            rows = pl.ds(cut * 32, 32)
            load(spec_hbm.at[part, away + chan, rows], wide_ref.at[chan, rows])
    if part == 0:
        for chan in range(2):
            load(spec_hbm.at[1, away + chan, pl.ds(0, 8)], lead_ref.at[chan])
    for chan in range(2):
        for cut in range(2):
            rows = pl.ds(cut * 32, 32)
            loads[2 * chan + cut].wait()
            send_ref[chan, rows] = wide_ref[chan, rows].astype(BF16)
            if part == 1:
                stores.append(
                    pltpu.make_async_copy(
                        send_ref.at[chan, rows], send_hbm.at[chan, rows], out_sems.at[2 * chan + cut]
                    )
                )
                stores[-1].start()
    if part == 0:
        for copy in loads[4:]:
            copy.wait()
        firsts = [wide_ref[chan, 0:1, :] for chan in range(2)] + [lead_ref[chan, 0:1, :] for chan in range(2)]
        rows_ref[...] = jnp.concatenate(firsts + [jnp.zeros((12, COLS), F32)], 0).astype(BF16)
    for copy in stores:
        copy.wait()


def filter_send(part, spec, half, ahead=None):
    anywhere = pl.BlockSpec(memory_space=pl.ANY)
    first = part == 0
    return pl.pallas_call(
        functools.partial(filter_send_body, part),
        in_specs=[pl.BlockSpec(memory_space=pltpu.SMEM), anywhere] + ([] if first else [anywhere]),
        out_specs=[pl.BlockSpec(memory_space=pltpu.VMEM)] * 2 if first else [anywhere],
        out_shape=[pltpu.VMEM((2, PER, COLS), BF16), jax.ShapeDtypeStruct((16, COLS), BF16)]
        if first
        else [jax.ShapeDtypeStruct((2, PER, COLS), BF16)],
        scratch_shapes=[
            pltpu.VMEM((2, PER, COLS), F32),
            pltpu.SemaphoreType.DMA((6,)),
        ]
        + (
            [pltpu.VMEM((2, 8, COLS), F32)]
            if first
            else [pltpu.VMEM((2, PER, COLS), BF16), pltpu.SemaphoreType.DMA((4,))]
        ),
        compiler_params=pltpu.CompilerParams(vmem_limit_bytes=(61 if first else 59) * 1024 * 1024),
        cost_estimate=pl.CostEstimate(flops=0, bytes_accessed=1_700_000, transcendentals=0),
        name="filter_send",
    )(*([half, spec] if first else [half, spec, ahead]))


def row_forward_body(
    x_ref, table_ref, base_ref, phase_ref, order_ref, out_ref, turned_ref,
):
    for chan in range(4):
        turned_ref[chan * LANES : (chan + 1) * LANES, :] = lax.dot_general(
            order_ref[...],
            x_ref[:, chan].reshape(HALF, LANES),
            (((1,), (1,)), ((), ())),
            preferred_element_type=F32,
        ).astype(BF16)

    lane = lax.broadcasted_iota(jnp.int32, (LANES, LANES), 1)
    first = lane < PER
    lead = lane % PER == 0
    base = base_ref[0]
    turned = pltpu.roll(base, PER, 1)
    own = jnp.where(first, base, turned), jnp.where(first, turned, base)

    def emit(place, real, imag):
        out_ref[place, 0] = real.astype(BF16)
        out_ref[place, 1] = imag.astype(BF16)

    high = []
    for block in range(BLOCKS):
        if block % 2 == 0:
            sums = jnp.dot(
                turned_ref[...], table_ref[:, block * LANES : (block + 2) * LANES], preferred_element_type=F32
            )
        cosine, sine = rotate(
            *own, base_ref[1, :, block : block + 1], base_ref[2, :, block : block + 1]
        )
        cosine, sine = rotate(cosine, sine, phase_ref[0, block], phase_ref[1, block])
        for pair in range(2):
            lanes = slice(block % 2 * LANES, block % 2 * LANES + LANES)
            upper = sums[pair * 256 : pair * 256 + 128, lanes]
            lower = sums[pair * 256 + 128 : pair * 256 + 256, lanes]
            real = jnp.where(first, upper, pltpu.roll(lower, PER, 1))
            imag = jnp.where(first, pltpu.roll(upper, PER, 1), lower)
            real, imag = rotate(real, imag, cosine, -sine)
            if pair == 0:
                emit(block, real, imag)
            else:
                high.append((real, imag))
        if block > 0:
            emit(16 - block, *(jnp.where(lead, new, old) for new, old in zip(high[block], high[block - 1])))
    emit(8, *(jnp.where(lead, new, old) for new, old in zip(high[0], high[7])))


def row_forward(x, table, base, phase, order):
    inside = pl.BlockSpec(memory_space=pltpu.VMEM)
    block = (16, 2, LANES, LANES)
    return pl.pallas_call(
        row_forward_body,
        in_specs=[inside] * 5,
        out_specs=inside,
        out_shape=jax.ShapeDtypeStruct(block, BF16),
        scratch_shapes=[
            pltpu.VMEM((4 * LANES, HALF), BF16),
        ],
        compiler_params=pltpu.CompilerParams(vmem_limit_bytes=16 * 1024 * 1024),
        cost_estimate=pl.CostEstimate(flops=1_100_000_000, bytes_accessed=5_000_000, transcendentals=0),
        name="row_forward",
    )(x, table, base, phase, order)


def filter_body(half_ref, own_ref, early_ref, late_ref, extra_ref, moves_ref, out_ref):
    for part in range(2):
        own = own_ref[part].reshape(LANES, own_ref.shape[3]).astype(BF16)
        got = (early_ref, late_ref)[part][...].reshape(LANES, early_ref.shape[2])
        total = None
        for source, low, high in ((own, 0, 128), (got, 128, 256), (extra_ref[...], 256, 272)):
            term = lax.dot_general(
                source, moves_ref[part, low:high, :], (((0,), (0,)), ((), ())), preferred_element_type=F32
            )
            total = term if total is None else total + term
        out_ref[0, part] = total[:, :LANES].astype(BF16)
        out_ref[1, part] = total[:, LANES:].astype(BF16)


def filter_layout(spec, half, early, late, extra, moves):
    step = 512
    return pl.pallas_call(
        filter_body,
        grid_spec=pltpu.PrefetchScalarGridSpec(
            num_scalar_prefetch=1,
            grid=(COLS // step,),
            in_specs=[
                pl.BlockSpec((2, 2, PER, step), lambda i, half: (0, half[0], 0, i)),
                pl.BlockSpec((2, PER, step), lambda i, half: (0, 0, i)),
                pl.BlockSpec((2, PER, step), lambda i, half: (0, 0, i)),
                pl.BlockSpec((16, step), lambda i, half: (0, i)),
                pl.BlockSpec((2, 272, 256), lambda i, half: (0, 0, 0)),
            ],
            out_specs=pl.BlockSpec((2, 2, step, LANES), lambda i, half: (0, 0, i, 0)),
        ),
        out_shape=jax.ShapeDtypeStruct((2, 2, COLS, LANES), BF16),
        compiler_params=pltpu.CompilerParams(vmem_limit_bytes=55 * 1024 * 1024),
        cost_estimate=pl.CostEstimate(flops=600_000_000, bytes_accessed=5_000_000, transcendentals=0),
        name="filter_layout",
    )(half, spec, early, late, extra, moves)


def column_body(
    y_ref, filt_ref, step_ref, mid_ref, within_ref, between_ref, special_ref, out_ref, turn_ref, work_ref,
):
    special = special_ref[...] > 0.5

    def outer_forward(step):
        rows = slice(step * 16, step * 16 + 16)
        parts = [[], [], [], []]
        for block in range(16):
            real = y_ref[block, 0, rows, :].astype(F32)
            imag = y_ref[block, 1, rows, :].astype(F32)
            cosine, sine = rotate(
                within_ref[0, rows, :],
                within_ref[1, rows, :],
                between_ref[0, block : block + 1, :],
                between_ref[1, block : block + 1, :],
            )
            turn_ref[0, block, rows, :] = cosine
            turn_ref[1, block, rows, :] = sine
            parts[0].append(real)
            parts[1].append(jnp.where(special, 0.0, imag))
            parts[2].append(jnp.where(special, imag * cosine, real))
            parts[3].append(jnp.where(special, imag * sine, imag))
        for side in range(2):
            data = [
                jnp.concatenate(
                    [x[half * 8 : half * 8 + 8] for x in parts[2 * side] + parts[2 * side + 1]], 0
                ).astype(BF16)
                for half in range(2)
            ]
            sums = jnp.dot(step_ref[side], jnp.concatenate(data, 1), preferred_element_type=F32)
            for part in range(2):
                for group in range(16):
                    for half in range(2):
                        at = group * LANES + step * 16 + half * 8
                        work_ref[2 * side + part, at : at + 8, :] = sums[
                            part * LANES + group * 8 : part * LANES + group * 8 + 8,
                            half * LANES : (half + 1) * LANES,
                        ]

    def inner_step(step):
        rows = slice(step * LANES, (step + 1) * LANES)
        mid = [[mid_ref[part, side, :, step : step + 1] for part in range(2)] for side in range(2)]
        sides = []
        for side in range(2):
            real, imag = rotate(
                work_ref[2 * side, rows, :], work_ref[2 * side + 1, rows, :], mid[side][0], -mid[side][1]
            )
            sides.append(jnp.concatenate([real.astype(BF16), imag.astype(BF16)], 0))
        spectrum = jnp.dot(step_ref[4], jnp.concatenate(sides, 1), preferred_element_type=F32)
        sides = []
        for side in range(2):
            lanes = slice(side * LANES, (side + 1) * LANES)
            real, imag = rotate(
                spectrum[:LANES, lanes],
                spectrum[LANES:, lanes],
                filt_ref[side, 0, rows, :].astype(F32),
                filt_ref[side, 1, rows, :].astype(F32),
            )
            sides.append(jnp.concatenate([real.astype(BF16), imag.astype(BF16)], 0))
        middle = jnp.dot(step_ref[5], jnp.concatenate(sides, 1), preferred_element_type=F32)
        for side in range(2):
            lanes = slice(side * LANES, (side + 1) * LANES)
            real, imag = rotate(middle[:LANES, lanes], middle[LANES:, lanes], mid[side][0], mid[side][1])
            work_ref[2 * side, rows, :] = real
            work_ref[2 * side + 1, rows, :] = imag

    def outer_inverse(step):
        rows = slice(step * 16, step * 16 + 16)
        sums = []
        for side in range(2):
            data = []
            for half in range(2):
                pieces = []
                for part in range(2):
                    for group in range(16):
                        at = group * LANES + step * 16 + half * 8
                        pieces.append(work_ref[2 * side + part, at : at + 8, :])
                data.append(jnp.concatenate(pieces, 0).astype(BF16))
            sums.append(jnp.dot(step_ref[2 + side], jnp.concatenate(data, 1), preferred_element_type=F32))
        near, far = sums
        for block in range(16):

            def both(sums, part):
                at = part * LANES + block * 8
                return jnp.concatenate([sums[at : at + 8, :LANES], sums[at : at + 8, LANES:]], 0)

            near_re, near_im, far_re, far_im = both(near, 0), both(near, 1), both(far, 0), both(far, 1)
            cosine, sine = turn_ref[0, block, rows, :], turn_ref[1, block, rows, :]
            total_re, total_im = near_re + far_re, near_im + far_im
            real = jnp.where(special, near_re, total_re * cosine - total_im * sine)
            imag = jnp.where(special, far_re, total_im) * cosine + jnp.where(special, far_im, total_re) * sine
            out_ref[block, 0, rows, :] = real.astype(BF16)
            out_ref[block, 1, rows, :] = imag.astype(BF16)

    for step in range(8):
        outer_forward(step)
    for step in range(16):
        inner_step(step)
    for step in range(8):
        outer_inverse(step)


def column_step(y, filt, steps, mid, within, between, special):
    inside = pl.BlockSpec(memory_space=pltpu.VMEM)
    return pl.pallas_call(
        column_body,
        in_specs=[inside] * 7,
        out_specs=inside,
        out_shape=jax.ShapeDtypeStruct((16, 2, LANES, LANES), BF16),
        scratch_shapes=[pltpu.VMEM((2, 16, LANES, LANES), F32), pltpu.VMEM((4, COLS, LANES), F32)],
        compiler_params=pltpu.CompilerParams(vmem_limit_bytes=24 * 1024 * 1024),
        cost_estimate=pl.CostEstimate(flops=2_000_000_000, bytes_accessed=5_000_000, transcendentals=0),
        name="column_step",
    )(y, filt, steps, mid, within, between, special)


def row_inverse_body(z_ref, table_ref, order_ref, out_ref, split_ref):
    lane = lax.broadcasted_iota(jnp.int32, (LANES, LANES), 1)
    first = lane < PER
    lead = lane % PER == 0
    for pair in range(2):
        for block in range(BLOCKS):
            parts = []
            for part in range(2):
                if pair == 0:
                    values = z_ref[block, part]
                else:
                    values = jnp.where(lead, z_ref[16 - block if block else 8, part], z_ref[15 - block, part])
                parts.append(values.astype(F32))
            real, imag = parts
            lanes = slice(block * LANES, (block + 1) * LANES)
            split_ref[pair * 256 : pair * 256 + 128, lanes] = jnp.where(
                first, real, pltpu.roll(imag, PER, 1)
            ).astype(BF16)
            split_ref[pair * 256 + 128 : pair * 256 + 256, lanes] = jnp.where(
                first, pltpu.roll(real, PER, 1), imag
            ).astype(BF16)
        sums = lax.dot_general(
            table_ref[...],
            split_ref[pair * 256 : (pair + 1) * 256, :],
            (((1,), (1,)), ((), ())),
            preferred_element_type=F32,
        ) * (1.0 / TOTAL)
        for copy in range(2):
            own = sums[:, copy * LANES : (copy + 1) * LANES].astype(BF16)
            own = jnp.dot(own, order_ref[...], preferred_element_type=F32).astype(BF16)
            for row in range(8):
                out_ref[row, 2 * pair + copy] = own[row * 64 : (row + 1) * 64]


def row_inverse(z, table, order):
    inside = pl.BlockSpec(memory_space=pltpu.VMEM)
    return pl.pallas_call(
        row_inverse_body,
        in_specs=[inside] * 3,
        out_specs=inside,
        out_shape=jax.ShapeDtypeStruct((8, 4, 64, LANES), BF16),
        scratch_shapes=[pltpu.VMEM((4 * LANES, ROWS), BF16)],
        compiler_params=pltpu.CompilerParams(vmem_limit_bytes=16 * 1024 * 1024),
        cost_estimate=pl.CostEstimate(flops=1_100_000_000, bytes_accessed=4_000_000, transcendentals=0),
        name="row_inverse",
    )(z, table, order)


def turn(first, second, modulus):
    angle = ((first * second) % modulus).astype(F32) * (TWO_PI / modulus)
    return jnp.stack([jnp.cos(angle), jnp.sin(angle)])


def per_device(gate_out, gate_in, values, filter_spec, skip):
    col = lax.axis_index("col")
    low_side = col < 8
    table = jnp.asarray(row_table())

    order = jnp.asarray(place_moves())

    half = jnp.where(low_side, 0, 1).astype(jnp.int32)[None]
    mirror = [(i, 15 - i) for i in range(16)]
    early_half, first_rows = filter_send(0, filter_spec, half)
    early = lax.ppermute(early_half, "col", mirror)
    extra = lax.ppermute(first_rows, "col", [(i, 16 - i if i % 8 else 8 - i) for i in range(16)])
    early_half, gate_in = lax.optimization_barrier((early_half, gate_in))
    gated = gate_in.astype(F32) * values.astype(F32)
    gated = gated.astype(BF16)
    x = lax.all_to_all(gated, "row", split_axis=0, concat_axis=0, tiled=True)
    late = lax.ppermute(filter_send(1, filter_spec, half, gated)[0], "col", mirror)
    moves = jnp.where(low_side, filter_moves()[0], filter_moves()[1])
    filt = filter_layout(filter_spec, half, early, late, extra, moves)

    lane = jnp.arange(LANES, dtype=jnp.int32) % PER
    all_k1 = (PER * jnp.arange(BLOCKS, dtype=jnp.int32))[:, None, None] + lane[None, None, :]
    phase = turn(all_k1, col, ROWS * 16)
    y = row_forward(x.reshape(8, 4, 64, LANES), table, twist_base(), phase, order)
    y = lax.all_to_all(y, "col", split_axis=0, concat_axis=0, tiled=True)

    own_k1 = PER * jnp.where(low_side, col, jnp.where(lane == 0, (16 - col) % 8, 15 - col)) + lane
    special = own_k1 == 0
    turn_k1 = jnp.where(special, -HALF, own_k1)
    within = turn(jnp.asarray(place_order(), jnp.int32)[:, None], turn_k1[None, :], TOTAL)
    between = turn(jnp.arange(16, dtype=jnp.int32)[:, None], turn_k1[None, :], ROWS * 16)
    mid = turn(jnp.asarray(middle_index()), 1, COLS)
    steps = jnp.asarray(step_tables()) * (col >= 0).astype(BF16)
    z = column_step(y, filt, steps, mid, within, between, special.astype(F32)[None, :])
    z = lax.all_to_all(z, "col", split_axis=0, concat_axis=0, tiled=True)

    convolved = row_inverse(z, table, order).reshape(32, 64, LANES)
    convolved = lax.all_to_all(convolved, "row", split_axis=0, concat_axis=0, tiled=True)
    gated = gate_in.astype(F32) * values.astype(F32)
    return gate_out.astype(F32) * (convolved.astype(F32) + skip[:, None, None] * gated)


def solution(mesh):
    return jax.shard_map(
        per_device,
        mesh=mesh,
        in_specs=(
            P(None, "row", "col"),
            P(None, "row", "col"),
            P(None, "row", "col"),
            P(None, "row", "col", None),
            P(),
        ),
        out_specs=P(None, "row", "col"),
        check_vma=False,
    )
```

```python
import functools
import math

import jax
import jax.numpy as jnp
import ml_dtypes
import numpy as np
from jax import lax
from jax.experimental import pallas as pl
from jax.experimental.pallas import tpu as pltpu
from jax.sharding import PartitionSpec as P

ROWS = 1024
COLS = 2048
OUTER = 64
INNER = 32
HALF = ROWS // 2
TOTAL = ROWS * COLS
LANES = 128
BLOCKS = 8
PER = HALF // BLOCKS
TWO_PI = 2.0 * math.pi
BF16 = jnp.bfloat16
F32 = jnp.float32


def grid_angle(first, second, modulus):
    product = (np.asarray(first, np.int64)[:, None] * np.asarray(second, np.int64)[None, :]) % modulus
    return product.astype(np.float32) * np.float32(TWO_PI / modulus)


def narrow(array):
    return np.asarray(array, np.float32).astype(ml_dtypes.bfloat16)


def row_table():
    angle = grid_angle(np.arange(HALF), np.arange(HALF), ROWS)
    cosines, sines = np.cos(angle), -np.sin(angle)
    sines[:, 0] = 1.0 - 2.0 * (np.arange(HALF) % 2)
    parts = np.stack([cosines, sines], 0).reshape(2, HALF, BLOCKS, PER).transpose(1, 2, 0, 3)
    return narrow(parts.reshape(HALF, BLOCKS * 2 * PER))


def pair_order(table, first, second):
    rows, cols = table.shape[0] // 2, table.shape[1] // 2
    out = np.zeros((2, rows // first, 2, first, 2, cols // second, 2, second), np.float32)
    for which in range(2):
        out[:, :, which, :, :, :, which, :] = table.reshape(2, rows // first, first, 2, cols // second, second)
    return out.reshape(4 * rows, 4 * cols)


def outer_tables():
    near = grid_angle(np.arange(OUTER), np.arange(OUTER), OUTER)
    far = grid_angle(np.arange(OUTER) + 1, np.arange(OUTER), OUTER)
    c, s, cm, sm = np.cos(near), np.sin(near), np.cos(far), np.sin(far)
    return [
        pair_order(np.block([[c, s], [-s, c]]), 1, 4),
        pair_order(np.block([[cm, -sm], [-sm, -cm]]), 1, 4),
        pair_order(np.block([[c.T, -s.T], [s.T, c.T]]), 4, 1),
        pair_order(np.block([[cm.T, -sm.T], [-sm.T, -cm.T]]), 4, 1),
    ]


def inner_tables():
    angle = grid_angle(np.arange(INNER), np.arange(INNER), INNER)
    c, s = np.cos(angle), np.sin(angle)
    spread = np.zeros((2, 4, INNER, 2, INNER // 2, 4, 2), np.float32)
    for k in range(4):
        spread[:, k, :, :, :, k, :] = np.block([[c, s], [-s, c]]).reshape(2, INNER, 2, INNER // 2, 2)
    spread = spread.reshape(256, 256)
    return [spread, spread.T]


def step_tables():
    return narrow(np.stack(outer_tables() + inner_tables()))


def middle_index():
    product = np.arange(OUTER + 1)[:, None] * np.arange(INNER)[None, :]
    sides = []
    for side in range(2):
        own = product[side : side + OUTER].reshape(16, 4, 16, 2).transpose(0, 2, 1, 3).reshape(16, LANES).T
        sides.append(np.pad(own, ((0, 0), (0, LANES - 16))))
    return np.stack(sides).astype(np.int32)


def place_order():
    return np.arange(LANES).reshape(4, INNER).T.reshape(-1)


def place_moves():
    return narrow(np.eye(LANES)[place_order()])


def twist_base():
    angle = grid_angle(place_order(), np.arange(PER), TOTAL)
    steps = np.pad(grid_angle(place_order(), PER * np.arange(BLOCKS), TOTAL), ((0, 0), (0, LANES - BLOCKS)))
    own = np.concatenate([np.cos(angle), np.sin(angle)], 1)
    return np.stack([own, np.cos(steps), np.sin(steps)]).astype(np.float32)


def filter_moves():
    moves = np.zeros((2, 2, 272, 256), np.float32)
    for copy in range(2):
        for e in range(PER):
            here, there, lane = copy * PER + e, copy * PER + (PER - e) % PER, copy * PER + e
            moves[0, :, here, lane] = 1.0
            moves[1, :, there, LANES + lane] = 1.0
            if e > 0:
                moves[0, :, LANES + there, LANES + lane] = 1.0
                moves[1, :, LANES + here, lane] = 1.0
            else:
                for part in range(2):
                    moves[0, part, 256 + 2 * part + copy, LANES + lane] = 1.0
                    moves[1, part, 256 + 2 * part + copy, lane] = 1.0
    return narrow(moves)


def rotate(real, imag, cosine, sine):
    return real * cosine - imag * sine, imag * cosine + real * sine


def filter_send_body(part, *refs):
    if part == 0:
        half_ref, spec_hbm, send_ref, rows_ref, wide_ref, in_sems, lead_ref = refs
    else:
        half_ref, spec_hbm, ahead_ref, send_hbm, wide_ref, in_sems, send_ref, out_sems = refs
    away = 2 * (1 - half_ref[0])
    loads, stores = [], []

    def load(source, target):
        loads.append(pltpu.make_async_copy(source, target, in_sems.at[len(loads)]))
        loads[-1].start()

    for chan in range(2):
        for cut in range(2):
            rows = pl.ds(cut * 32, 32)
            load(spec_hbm.at[part, away + chan, rows], wide_ref.at[chan, rows])
    if part == 0:
        for chan in range(2):
            load(spec_hbm.at[1, away + chan, pl.ds(0, 8)], lead_ref.at[chan])
    for chan in range(2):
        for cut in range(2):
            rows = pl.ds(cut * 32, 32)
            loads[2 * chan + cut].wait()
            send_ref[chan, rows] = wide_ref[chan, rows].astype(BF16)
            if part == 1:
                stores.append(
                    pltpu.make_async_copy(
                        send_ref.at[chan, rows], send_hbm.at[chan, rows], out_sems.at[2 * chan + cut]
                    )
                )
                stores[-1].start()
    if part == 0:
        for copy in loads[4:]:
            copy.wait()
        firsts = [wide_ref[chan, 0:1, :] for chan in range(2)] + [lead_ref[chan, 0:1, :] for chan in range(2)]
        rows_ref[...] = jnp.concatenate(firsts + [jnp.zeros((12, COLS), F32)], 0).astype(BF16)
    for copy in stores:
        copy.wait()


def filter_send(part, spec, half, ahead=None):
    anywhere = pl.BlockSpec(memory_space=pl.ANY)
    first = part == 0
    return pl.pallas_call(
        functools.partial(filter_send_body, part),
        in_specs=[pl.BlockSpec(memory_space=pltpu.SMEM), anywhere] + ([] if first else [anywhere]),
        out_specs=[pl.BlockSpec(memory_space=pltpu.VMEM)] * 2 if first else [anywhere],
        out_shape=[pltpu.VMEM((2, PER, COLS), BF16), jax.ShapeDtypeStruct((16, COLS), BF16)]
        if first
        else [jax.ShapeDtypeStruct((2, PER, COLS), BF16)],
        scratch_shapes=[
            pltpu.VMEM((2, PER, COLS), F32),
            pltpu.SemaphoreType.DMA((6,)),
        ]
        + (
            [pltpu.VMEM((2, 8, COLS), F32)]
            if first
            else [pltpu.VMEM((2, PER, COLS), BF16), pltpu.SemaphoreType.DMA((4,))]
        ),
        compiler_params=pltpu.CompilerParams(vmem_limit_bytes=(61 if first else 59) * 1024 * 1024),
        cost_estimate=pl.CostEstimate(flops=0, bytes_accessed=1_700_000, transcendentals=0),
        name="filter_send",
    )(*([half, spec] if first else [half, spec, ahead]))


def row_forward_body(
    x_ref, table_ref, base_ref, phase_ref, order_ref, out_ref, turned_ref,
):
    for chan in range(4):
        turned_ref[chan * LANES : (chan + 1) * LANES, :] = lax.dot_general(
            order_ref[...],
            x_ref[:, chan].reshape(HALF, LANES),
            (((1,), (1,)), ((), ())),
            preferred_element_type=F32,
        ).astype(BF16)

    lane = lax.broadcasted_iota(jnp.int32, (LANES, LANES), 1)
    first = lane < PER
    lead = lane % PER == 0
    base = base_ref[0]
    turned = pltpu.roll(base, PER, 1)
    own = jnp.where(first, base, turned), jnp.where(first, turned, base)

    def emit(place, real, imag):
        out_ref[place, 0] = real.astype(BF16)
        out_ref[place, 1] = imag.astype(BF16)

    high = []
    for block in range(BLOCKS):
        if block % 2 == 0:
            sums = jnp.dot(
                turned_ref[...], table_ref[:, block * LANES : (block + 2) * LANES], preferred_element_type=F32
            )
        cosine, sine = rotate(
            *own, base_ref[1, :, block : block + 1], base_ref[2, :, block : block + 1]
        )
        cosine, sine = rotate(cosine, sine, phase_ref[0, block], phase_ref[1, block])
        for pair in range(2):
            lanes = slice(block % 2 * LANES, block % 2 * LANES + LANES)
            upper = sums[pair * 256 : pair * 256 + 128, lanes]
            lower = sums[pair * 256 + 128 : pair * 256 + 256, lanes]
            real = jnp.where(first, upper, pltpu.roll(lower, PER, 1))
            imag = jnp.where(first, pltpu.roll(upper, PER, 1), lower)
            real, imag = rotate(real, imag, cosine, -sine)
            if pair == 0:
                emit(block, real, imag)
            else:
                high.append((real, imag))
        if block > 0:
            emit(16 - block, *(jnp.where(lead, new, old) for new, old in zip(high[block], high[block - 1])))
    emit(8, *(jnp.where(lead, new, old) for new, old in zip(high[0], high[7])))


def row_forward(x, table, base, phase, order):
    inside = pl.BlockSpec(memory_space=pltpu.VMEM)
    block = (16, 2, LANES, LANES)
    return pl.pallas_call(
        row_forward_body,
        in_specs=[inside] * 5,
        out_specs=inside,
        out_shape=jax.ShapeDtypeStruct(block, BF16),
        scratch_shapes=[
            pltpu.VMEM((4 * LANES, HALF), BF16),
        ],
        compiler_params=pltpu.CompilerParams(vmem_limit_bytes=16 * 1024 * 1024),
        cost_estimate=pl.CostEstimate(flops=1_100_000_000, bytes_accessed=5_000_000, transcendentals=0),
        name="row_forward",
    )(x, table, base, phase, order)


def filter_body(
    half_ref, spec_hbm, early_hbm, late_hbm, extra_ref, moves_ref, out_ref, own_ref, early_ref, late_ref, sems,
):
    step = 512
    copies = []
    for index in range(COLS // step):
        cols = pl.ds(index * step, step)
        copies.append([])
        for source, target in (
            (spec_hbm.at[:, pl.ds(2 * half_ref[0], 2), :, cols], own_ref.at[:, :, :, cols]),
            (early_hbm.at[:, :, cols], early_ref.at[:, :, cols]),
            (late_hbm.at[:, :, cols], late_ref.at[:, :, cols]),
        ):
            copies[index].append(pltpu.make_async_copy(source, target, sems.at[index, len(copies[index])]))
            copies[index][-1].start()
    for index in range(COLS // step):
        for copy in copies[index]:
            copy.wait()
        cols = slice(index * step, (index + 1) * step)
        for part in range(2):
            own = own_ref[part, :, :, cols].reshape(LANES, step).astype(BF16)
            got = (early_ref, late_ref)[part][:, :, cols].reshape(LANES, step)
            total = None
            for source, low, high in ((own, 0, 128), (got, 128, 256), (extra_ref[:, cols], 256, 272)):
                term = lax.dot_general(
                    source, moves_ref[part, low:high, :], (((0,), (0,)), ((), ())), preferred_element_type=F32
                )
                total = term if total is None else total + term
            out_ref[0, part, cols, :] = total[:, :LANES].astype(BF16)
            out_ref[1, part, cols, :] = total[:, LANES:].astype(BF16)


def filter_layout(spec, half, early, late, extra, moves):
    anywhere = pl.BlockSpec(memory_space=pl.ANY)
    inside = pl.BlockSpec(memory_space=pltpu.VMEM)
    return pl.pallas_call(
        filter_body,
        in_specs=[pl.BlockSpec(memory_space=pltpu.SMEM), anywhere, anywhere, anywhere, inside, inside],
        out_specs=inside,
        out_shape=pltpu.VMEM((2, 2, COLS, LANES), BF16),
        scratch_shapes=[
            pltpu.VMEM((2, 2, PER, COLS), F32),
            pltpu.VMEM((2, PER, COLS), BF16),
            pltpu.VMEM((2, PER, COLS), BF16),
            pltpu.SemaphoreType.DMA((4, 3)),
        ],
        compiler_params=pltpu.CompilerParams(vmem_limit_bytes=55 * 1024 * 1024),
        cost_estimate=pl.CostEstimate(flops=600_000_000, bytes_accessed=5_000_000, transcendentals=0),
        name="filter_layout",
    )(half, spec, early, late, extra, moves)


def column_body(
    y_ref, filt_ref, step_ref, mid_ref, within_ref, between_ref, special_ref, out_ref, turn_ref, work_ref,
):
    special = special_ref[...] > 0.5

    def outer_forward(step):
        rows = slice(step * 16, step * 16 + 16)
        parts = [[], [], [], []]
        for block in range(16):
            real = y_ref[block, 0, rows, :].astype(F32)
            imag = y_ref[block, 1, rows, :].astype(F32)
            cosine, sine = rotate(
                within_ref[0, rows, :],
                within_ref[1, rows, :],
                between_ref[0, block : block + 1, :],
                between_ref[1, block : block + 1, :],
            )
            turn_ref[0, block, rows, :] = cosine
            turn_ref[1, block, rows, :] = sine
            parts[0].append(real)
            parts[1].append(jnp.where(special, 0.0, imag))
            parts[2].append(jnp.where(special, imag * cosine, real))
            parts[3].append(jnp.where(special, imag * sine, imag))
        for side in range(2):
            data = [
                jnp.concatenate(
                    [x[half * 8 : half * 8 + 8] for x in parts[2 * side] + parts[2 * side + 1]], 0
                ).astype(BF16)
                for half in range(2)
            ]
            sums = jnp.dot(step_ref[side], jnp.concatenate(data, 1), preferred_element_type=F32)
            for part in range(2):
                for group in range(16):
                    for half in range(2):
                        at = group * LANES + step * 16 + half * 8
                        work_ref[2 * side + part, at : at + 8, :] = sums[
                            part * LANES + group * 8 : part * LANES + group * 8 + 8,
                            half * LANES : (half + 1) * LANES,
                        ]

    def inner_step(step):
        rows = slice(step * LANES, (step + 1) * LANES)
        mid = [[mid_ref[part, side, :, step : step + 1] for part in range(2)] for side in range(2)]
        sides = []
        for side in range(2):
            real, imag = rotate(
                work_ref[2 * side, rows, :], work_ref[2 * side + 1, rows, :], mid[side][0], -mid[side][1]
            )
            sides.append(jnp.concatenate([real.astype(BF16), imag.astype(BF16)], 0))
        spectrum = jnp.dot(step_ref[4], jnp.concatenate(sides, 1), preferred_element_type=F32)
        sides = []
        for side in range(2):
            lanes = slice(side * LANES, (side + 1) * LANES)
            real, imag = rotate(
                spectrum[:LANES, lanes],
                spectrum[LANES:, lanes],
                filt_ref[side, 0, rows, :].astype(F32),
                filt_ref[side, 1, rows, :].astype(F32),
            )
            sides.append(jnp.concatenate([real.astype(BF16), imag.astype(BF16)], 0))
        middle = jnp.dot(step_ref[5], jnp.concatenate(sides, 1), preferred_element_type=F32)
        for side in range(2):
            lanes = slice(side * LANES, (side + 1) * LANES)
            real, imag = rotate(middle[:LANES, lanes], middle[LANES:, lanes], mid[side][0], mid[side][1])
            work_ref[2 * side, rows, :] = real
            work_ref[2 * side + 1, rows, :] = imag

    def outer_inverse(step):
        rows = slice(step * 16, step * 16 + 16)
        sums = []
        for side in range(2):
            data = []
            for half in range(2):
                pieces = []
                for part in range(2):
                    for group in range(16):
                        at = group * LANES + step * 16 + half * 8
                        pieces.append(work_ref[2 * side + part, at : at + 8, :])
                data.append(jnp.concatenate(pieces, 0).astype(BF16))
            sums.append(jnp.dot(step_ref[2 + side], jnp.concatenate(data, 1), preferred_element_type=F32))
        near, far = sums
        for block in range(16):

            def both(sums, part):
                at = part * LANES + block * 8
                return jnp.concatenate([sums[at : at + 8, :LANES], sums[at : at + 8, LANES:]], 0)

            near_re, near_im, far_re, far_im = both(near, 0), both(near, 1), both(far, 0), both(far, 1)
            cosine, sine = turn_ref[0, block, rows, :], turn_ref[1, block, rows, :]
            total_re, total_im = near_re + far_re, near_im + far_im
            real = jnp.where(special, near_re, total_re * cosine - total_im * sine)
            imag = jnp.where(special, far_re, total_im) * cosine + jnp.where(special, far_im, total_re) * sine
            out_ref[block, 0, rows, :] = real.astype(BF16)
            out_ref[block, 1, rows, :] = imag.astype(BF16)

    for step in range(8):
        outer_forward(step)
    for step in range(16):
        inner_step(step)
    for step in range(8):
        outer_inverse(step)


def column_step(y, filt, steps, mid, within, between, special):
    inside = pl.BlockSpec(memory_space=pltpu.VMEM)
    return pl.pallas_call(
        column_body,
        in_specs=[inside] * 7,
        out_specs=inside,
        out_shape=jax.ShapeDtypeStruct((16, 2, LANES, LANES), BF16),
        scratch_shapes=[pltpu.VMEM((2, 16, LANES, LANES), F32), pltpu.VMEM((4, COLS, LANES), F32)],
        compiler_params=pltpu.CompilerParams(vmem_limit_bytes=24 * 1024 * 1024),
        cost_estimate=pl.CostEstimate(flops=2_000_000_000, bytes_accessed=5_000_000, transcendentals=0),
        name="column_step",
    )(y, filt, steps, mid, within, between, special)


def row_inverse_body(z_ref, table_ref, order_ref, out_ref, split_ref):
    lane = lax.broadcasted_iota(jnp.int32, (LANES, LANES), 1)
    first = lane < PER
    lead = lane % PER == 0
    for pair in range(2):
        for block in range(BLOCKS):
            parts = []
            for part in range(2):
                if pair == 0:
                    values = z_ref[block, part]
                else:
                    values = jnp.where(lead, z_ref[16 - block if block else 8, part], z_ref[15 - block, part])
                parts.append(values.astype(F32))
            real, imag = parts
            lanes = slice(block * LANES, (block + 1) * LANES)
            split_ref[pair * 256 : pair * 256 + 128, lanes] = jnp.where(
                first, real, pltpu.roll(imag, PER, 1)
            ).astype(BF16)
            split_ref[pair * 256 + 128 : pair * 256 + 256, lanes] = jnp.where(
                first, pltpu.roll(real, PER, 1), imag
            ).astype(BF16)
        sums = lax.dot_general(
            table_ref[...],
            split_ref[pair * 256 : (pair + 1) * 256, :],
            (((1,), (1,)), ((), ())),
            preferred_element_type=F32,
        ) * (1.0 / TOTAL)
        for copy in range(2):
            own = sums[:, copy * LANES : (copy + 1) * LANES].astype(BF16)
            own = jnp.dot(own, order_ref[...], preferred_element_type=F32).astype(BF16)
            for row in range(8):
                out_ref[row, 2 * pair + copy] = own[row * 64 : (row + 1) * 64]


def row_inverse(z, table, order):
    inside = pl.BlockSpec(memory_space=pltpu.VMEM)
    return pl.pallas_call(
        row_inverse_body,
        in_specs=[inside] * 3,
        out_specs=inside,
        out_shape=jax.ShapeDtypeStruct((8, 4, 64, LANES), BF16),
        scratch_shapes=[pltpu.VMEM((4 * LANES, ROWS), BF16)],
        compiler_params=pltpu.CompilerParams(vmem_limit_bytes=16 * 1024 * 1024),
        cost_estimate=pl.CostEstimate(flops=1_100_000_000, bytes_accessed=4_000_000, transcendentals=0),
        name="row_inverse",
    )(z, table, order)


def turn(first, second, modulus):
    angle = ((first * second) % modulus).astype(F32) * (TWO_PI / modulus)
    return jnp.stack([jnp.cos(angle), jnp.sin(angle)])


def per_device(gate_out, gate_in, values, filter_spec, skip):
    col = lax.axis_index("col")
    low_side = col < 8
    table = jnp.asarray(row_table())

    order = jnp.asarray(place_moves())

    half = jnp.where(low_side, 0, 1).astype(jnp.int32)[None]
    mirror = [(i, 15 - i) for i in range(16)]
    early_half, first_rows = filter_send(0, filter_spec, half)
    early = lax.ppermute(early_half, "col", mirror)
    extra = lax.ppermute(first_rows, "col", [(i, 16 - i if i % 8 else 8 - i) for i in range(16)])
    early_half, gate_in = lax.optimization_barrier((early_half, gate_in))
    gated = gate_in.astype(F32) * values.astype(F32)
    gated = gated.astype(BF16)
    x = lax.all_to_all(gated, "row", split_axis=0, concat_axis=0, tiled=True)
    late = lax.ppermute(filter_send(1, filter_spec, half, gated)[0], "col", mirror)
    moves = jnp.where(low_side, filter_moves()[0], filter_moves()[1])
    filt = filter_layout(filter_spec, half, early, late, extra, moves)

    lane = jnp.arange(LANES, dtype=jnp.int32) % PER
    all_k1 = (PER * jnp.arange(BLOCKS, dtype=jnp.int32))[:, None, None] + lane[None, None, :]
    phase = turn(all_k1, col, ROWS * 16)
    y = row_forward(x.reshape(8, 4, 64, LANES), table, twist_base(), phase, order)
    y = lax.all_to_all(y, "col", split_axis=0, concat_axis=0, tiled=True)

    own_k1 = PER * jnp.where(low_side, col, jnp.where(lane == 0, (16 - col) % 8, 15 - col)) + lane
    special = own_k1 == 0
    turn_k1 = jnp.where(special, -HALF, own_k1)
    within = turn(jnp.asarray(place_order(), jnp.int32)[:, None], turn_k1[None, :], TOTAL)
    between = turn(jnp.arange(16, dtype=jnp.int32)[:, None], turn_k1[None, :], ROWS * 16)
    mid = turn(jnp.asarray(middle_index()), 1, COLS)
    steps = jnp.asarray(step_tables()) * (col >= 0).astype(BF16)
    z = column_step(y, filt, steps, mid, within, between, special.astype(F32)[None, :])
    z = lax.all_to_all(z, "col", split_axis=0, concat_axis=0, tiled=True)

    convolved = row_inverse(z, table, order).reshape(32, 64, LANES)
    convolved = lax.all_to_all(convolved, "row", split_axis=0, concat_axis=0, tiled=True)
    gated = gate_in.astype(F32) * values.astype(F32)
    return gate_out.astype(F32) * (convolved.astype(F32) + skip[:, None, None] * gated)


def solution(mesh):
    return jax.shard_map(
        per_device,
        mesh=mesh,
        in_specs=(
            P(None, "row", "col"),
            P(None, "row", "col"),
            P(None, "row", "col"),
            P(None, "row", "col", None),
            P(),
        ),
        out_specs=P(None, "row", "col"),
        check_vma=False,
    )
```
